512 devices in a mesh: blk: 128 (over z, y, core), rep: 4 (over x).
Axes of the slice: x: 4, y: 8, z: 8, core: 2. Of those that a mesh axis runs over, the one named last changes fastest.
Arguments:
- pair_blocks: bfloat16 [128, 128, 128, 128], P('blk', 'rep'), may hold values from -6 to 6
- kept_pairs: int32 [128, 2], replicated, may hold values from 0 to 63, as said below
- owner: int32 [64, 64], replicated, may hold values from -1 to 127, as said below
- norm_gain: float32 [128], replicated, may hold values from 0.5 to 1.5
- norm_offset: float32 [128], replicated, may hold values from -3 to 3
- w_query: bfloat16 [128, 128], replicated
- w_key: bfloat16 [128, 128], replicated
- w_value: bfloat16 [128, 128], replicated, may hold values from -0.5 to 0.5
- w_gate: bfloat16 [128, 128], replicated, may hold values from -0.5 to 0.5
- gate_bias: float32 [128], replicated, may hold values from -4 to 4
- w_bias: bfloat16 [128, 4], replicated, may hold values from -1 to 1
- w_out: bfloat16 [128, 128], replicated, may hold values from -0.5 to 0.5
Outputs:
- update: bfloat16 [128, 128, 128, 128], P('blk', 'rep')
The draws below stay inside these ranges and needn't reach their ends.
Inputs may be any that keep to these rules, and one draw needn't show every extreme that they name: `kept_pairs`: rows sorted by block row, then block column; no pair twice; every block row I keeps its diagonal block (I, I) and 1 to 3 blocks in all, some row exactly 3; a row of 2 or more blocks keeps column (I + 32) mod 64; block row I + 32 keeps the columns of block row I shifted by 64 / 2 modulo 64. owner[I, J] is the row of kept_pairs holding (I, J), -1 where the block is not kept.
All inputs are finite; a program needn't handle non-finite values.
Results may differ from the reference program's by a relative error of at most 0.011.
Values may be sent and summed in bfloat16 or wider, within the bound.
A program may use at most 64 MiB of HBM per device.

```python
import jax
import jax.numpy as jnp
from jax import lax

C = 128
H = 4
BLOCK = 128
ROW_MOST = 3
HH = 128
KEPT = 128
NB = 64


def block_layout(key):
    key = jax.random.fold_in(key, 21)
    first, second = jax.random.split(key)
    half = NB // 2
    moves = max(half // 4, 1)
    rows_half = jnp.arange(half, dtype=jnp.int32)
    rank = jax.random.permutation(first, half).astype(jnp.int32)
    counts = 2 + (rank < moves).astype(jnp.int32) - ((rank >= moves) & (rank < 2 * moves)).astype(jnp.int32)
    step = jax.random.randint(second, (half,), 1, NB - 1).astype(jnp.int32)
    step = step + (step >= half).astype(jnp.int32)
    extra = ((rows_half + step) % NB).astype(jnp.int32)
    columns = jnp.arange(NB, dtype=jnp.int32)[None, :]
    keep_half = columns == rows_half[:, None]
    keep_half = keep_half | (counts[:, None] >= 2) & (columns == rows_half[:, None] + half)
    keep_half = keep_half | (counts[:, None] >= 3) & (columns == extra[:, None])
    keep = jnp.concatenate([keep_half, jnp.roll(keep_half, half, axis=1)], axis=0)
    flat = keep.reshape(-1).astype(jnp.int32)
    position = jnp.cumsum(flat) - 1
    owner_map = jnp.where(keep, position.reshape(NB, NB), -1).astype(jnp.int32)
    index = jnp.nonzero(flat, size=KEPT)[0].astype(jnp.int32)
    pairs = jnp.stack([index // NB, index % NB], axis=1).astype(jnp.int32)
    return (pairs, owner_map)


def draw_kept_pairs(key, part):
    pairs, owner_map = block_layout(key)
    return pairs


def draw_owner(key, part):
    pairs, owner_map = block_layout(key)
    return owner_map


def draw_w_query(key, part):
    key = jax.random.fold_in(key, 11)
    own = jax.random.normal(key, (C, HH), jnp.float32)
    weight = own * C ** (-0.5)
    return weight.astype(jnp.bfloat16)


def draw_w_key(key, part):
    key = jax.random.fold_in(key, 12)
    own = jax.random.normal(key, (C, HH), jnp.float32)
    weight = own * C ** (-0.5)
    return weight.astype(jnp.bfloat16)


def block_levels(own_key, dims, cuts, low, high):
    loudness, own = 1.0, jax.random.fold_in(own_key, 6)
    for axis_at, parts in cuts:
        heights = jnp.exp(jax.random.uniform(jax.random.fold_in(own, axis_at), (parts,), jnp.float32, low / len(cuts), high / len(cuts)))
        loudness = loudness * jnp.repeat(heights, dims[axis_at] // parts).reshape([-1 if axis == axis_at else 1 for axis in range(len(dims))])
    return loudness


def noise(stream_key, shape, deviation, bound, cuts=(), kind=jnp.bfloat16):
    level = block_levels(stream_key, shape, cuts, -0.22, 0.18) if cuts else 1.0
    array = jax.random.normal(stream_key, shape, jnp.float32) * deviation * level
    return jnp.minimum(jnp.maximum(array, -bound), bound).astype(kind)


def setup_inputs(seed: int = 0) -> dict:
    key_list = jax.random.split(jax.random.key(seed), 13)
    pair_blocks = noise(key_list[0], (KEPT, BLOCK, BLOCK, C), 1.0, 6.0, ((0, 128), (1, 4)))
    kept_pairs = draw_kept_pairs(jax.random.fold_in(key_list[12], 71), 0)
    owner = draw_owner(jax.random.fold_in(key_list[12], 71), 0)
    norm_gain = jnp.clip(1.0 + 0.1 * jax.random.normal(key_list[3], (C,), jnp.float32), 0.5, 1.5)
    norm_offset = noise(key_list[4], (C,), 0.3, 3.0, (), jnp.float32)
    w_query = draw_w_query(jax.random.fold_in(key_list[12], 71), 0)
    w_key = draw_w_key(jax.random.fold_in(key_list[12], 71), 0)
    w_value = noise(key_list[7], (C, HH), C ** -0.5, 0.5)
    w_gate = noise(key_list[8], (C, HH), C ** -0.5, 0.5)
    gate_bias = noise(key_list[9], (HH,), 1.0, 4.0, (), jnp.float32)
    w_bias = noise(key_list[10], (C, H), (C // 4) ** -0.5, 1.0)
    w_out = noise(key_list[11], (HH, C), HH ** -0.5, 0.5)
    return {"pair_blocks": pair_blocks, "kept_pairs": kept_pairs, "owner": owner, "norm_gain": norm_gain, "norm_offset": norm_offset, "w_query": w_query, "w_key": w_key, "w_value": w_value, "w_gate": w_gate, "gate_bias": gate_bias, "w_bias": w_bias, "w_out": w_out}


def norm_rows(pairs, gain, offset):
    values = pairs.astype(jnp.float32)
    center = lax.optimization_barrier(jnp.mean(values, axis=-1, keepdims=True))
    spread = lax.optimization_barrier(jnp.mean((values - center) ** 2, axis=-1, keepdims=True))
    return ((values - center) * lax.rsqrt(spread + 1e-05) * gain + offset).astype(jnp.bfloat16)

def project(feats, weight):
    flat = feats.reshape(-1, feats.shape[-1])
    result = jnp.dot(flat, weight, preferred_element_type=jnp.float32)
    return result.reshape(feats.shape[:-1] + (weight.shape[1],))

def reference(pair_blocks, kept_pairs, owner, norm_gain, norm_offset, w_query, w_key, w_value, w_gate, gate_bias, w_bias, w_out):
    heads = w_bias.shape[1]
    inner = w_query.shape[1]
    head_size = inner // heads
    width = pair_blocks.shape[1]
    kept = pair_blocks.shape[0]

    def side(block):
        normed = norm_rows(block, norm_gain, norm_offset)
        return (project(normed, w_key).astype(jnp.bfloat16), project(normed, w_value).astype(jnp.bfloat16), project(normed, w_bias).astype(jnp.bfloat16).transpose(2, 0, 1))
    key_all, value_all, bias_all = lax.map(side, pair_blocks)

    def single(slot):
        normed = norm_rows(pair_blocks[slot], norm_gain, norm_offset)
        query = (project(normed, w_query) * head_size ** (-0.5)).astype(jnp.bfloat16)
        gate = jax.nn.sigmoid(project(normed, w_gate) + gate_bias)
        row_i = kept_pairs[slot, 0]
        col_j = kept_pairs[slot, 1]
        members = owner[row_i]
        start = jnp.min(jnp.where(members >= 0, members, kept)).astype(jnp.int32)
        count = jnp.sum((members >= 0).astype(jnp.int32))
        offsets = jnp.arange(ROW_MOST, dtype=jnp.int32)
        index = jnp.clip(start + offsets, 0, kept - 1).astype(jnp.int32)
        valid = offsets < count
        keys = key_all[index].astype(jnp.float32).reshape(ROW_MOST, width, width, heads, head_size)
        values = value_all[index].astype(jnp.float32).reshape(ROW_MOST, width, width, heads, head_size)
        bias_slot = owner[col_j, kept_pairs[index, 1]]
        bias = jnp.where((bias_slot >= 0)[:, None, None, None], bias_all[jnp.clip(bias_slot, 0, kept - 1)], jnp.zeros((), jnp.bfloat16)).astype(jnp.float32)
        query4 = query.astype(jnp.float32).reshape(width, width, heads, head_size)
        scores = jnp.einsum('ijhd,rikhd->hijrk', query4, keys) + bias.transpose(1, 2, 0, 3)[:, None]
        scores = jnp.where(valid[None, None, None, :, None], scores, -1e+30)
        top = lax.optimization_barrier(jnp.max(scores, axis=(3, 4), keepdims=True))
        weights = jnp.exp(scores - top)
        total = lax.optimization_barrier(jnp.sum(weights, axis=(3, 4)))
        probs = lax.optimization_barrier(weights.astype(jnp.bfloat16)).astype(jnp.float32)
        attended = jnp.einsum('hijrk,rikhd->ijhd', probs, values) / total.transpose(1, 2, 0)[..., None]
        gated = (gate * attended.reshape(width, width, inner)).astype(jnp.bfloat16)
        return project(gated, w_out).astype(jnp.bfloat16)
    return lax.map(single, jnp.arange(kept, dtype=jnp.int32))
```

```python
import functools

import jax
import jax.numpy as jnp
from jax import lax
from jax.experimental import pallas as pl
from jax.experimental.pallas import tpu as pltpu
from jax.sharding import PartitionSpec as P

F32 = jnp.float32
BF = jnp.bfloat16
I32 = jnp.int32
MESH = pl.DeviceIdType.MESH
LOG2E = 1.4426950408889634
MASKED = -1e30

NZ, NY, NX = 8, 8, 4
PLANE = 2 * NY
KEPT = NZ * PLANE
ROWS = 32
W = 128
HEADS, HD = 4, 32
CHUNKS = 4
RC = ROWS // CHUNKS
Y_STEPS = (1, -1, 2, -2, 3, -3, 4)
Z_STEPS = (1, -1, 2, -2, 3, -3, 4)
X_STEPS = (1, -1, 2)


def dot(a, b):
    return jnp.dot(a, b, preferred_element_type=F32)


def dot_nt(a, b):
    return lax.dot_general(a, b, (((1,), (1,)), ((), ())), preferred_element_type=F32)


def dot_tn(a, b):
    return lax.dot_general(a, b, (((0,), (0,)), ((), ())), preferred_element_type=F32)


def norm_rows(x, gain, offset):
    v = x.astype(F32)
    d = v - jnp.mean(v, axis=-1, keepdims=True)
    s = jnp.mean(d * d, axis=-1, keepdims=True)
    return (d * lax.rsqrt(s + 1e-05) * gain + offset).astype(BF)


def row_members(kept, slot):
    row = kept[slot, 0]

    def same(step):
        other = slot + step
        inside = (other >= 0) & (other < KEPT)
        return inside & (kept[jnp.clip(other, 0, KEPT - 1), 0] == row)

    m1, m2, p1, p2 = same(-1), same(-2), same(1), same(2)
    first = jnp.where(m1, -1, 1)
    second = jnp.where(m1 & p1, 1, jnp.where(m2, -2, 2))
    return first, m1 | p1, second, (m1 & p1) | m2 | p2


def bias_wants(kept, owner, slot):
    first, has_first, second, has_second = row_members(kept, slot)
    col = kept[slot, 1]
    k1 = kept[jnp.clip(slot + first, 0, KEPT - 1), 1]
    k2 = kept[jnp.clip(slot + second, 0, KEPT - 1), 1]
    g0 = owner[col, col]
    g1 = jnp.where(has_first, owner[col, k1], -1)
    g2 = jnp.where(has_second, owner[col, k2], -1)
    diag = kept[slot, 0] == col
    one = jnp.where(diag, g1, g0)
    two = jnp.where(diag, g2, jnp.maximum(g1, g2))
    return diag, g0, g1, g2, one, two


def kernel(
    kept, owner, x_ref, gain_ref, offset_ref, wq_ref, wk_ref, wv_ref, wg_ref, gb_ref, wb_ref, wo_ref,
    out_ref,
    normed, plane, z_send, z_recv, picked, whole, nb0, nb1, nb2, nb3,
    q_t, gate_t, k_all, v_t, gated, bias_t, wqg_t, wv_t, gb_t, wb_rep,
    s0, s1, p0, p1, m0, m1,
    y_ss, y_rs, c_ss, c_rs, z_ss, z_rs, x_ss, x_rs, n_ss, n_rs,
):
    blk = lax.axis_index("blk")
    rep = lax.axis_index("rep")
    z = blk // PLANE
    y = (blk // 2) % NY
    core = blk % 2
    nbs = (nb0, nb1, nb2, nb3)

    def at_blk(b):
        return {"blk": (b + KEPT) % KEPT}

    def at_y(step):
        return {"blk": z * PLANE + ((y + step + NY) % NY) * 2 + core}

    def at_z(step):
        return {"blk": ((z + step + NZ) % NZ) * PLANE + y * 2 + core}

    def at_x(step):
        return {"rep": (rep + step + NX) % NX}

    mate = {"blk": blk + 1 - 2 * core}

    barrier = pltpu.get_barrier_semaphore()
    greeted = [at_y(s) for s in Y_STEPS] + [at_z(s) for s in Z_STEPS] + [at_x(s) for s in X_STEPS] + [mate]
    greeted += [at_blk(blk - 2 + 3 * core), at_blk(blk - 1 + 3 * core)]
    for device in greeted:
        pl.semaphore_signal(barrier, inc=1, device_id=device, device_id_type=MESH)

    def remote(src, dst, ss, rs, device):
        return pltpu.make_async_remote_copy(
            src_ref=src, dst_ref=dst, send_sem=ss, recv_sem=rs, device_id=device, device_id_type=MESH
        )

    def turned(w):
        return w.astype(F32).T.astype(BF)

    wqg_t[0:W] = turned(wq_ref[...])
    wqg_t[W:] = turned(wg_ref[...])
    wv_t[...] = turned(wv_ref[...])
    gb_t[...] = jnp.broadcast_to(gb_ref[...], (W, W)).T
    wb = wb_ref[...].astype(F32)
    wb_rep[...] = jnp.concatenate([jnp.broadcast_to(wb[:, h : h + 1], (W, ROWS)) for h in range(HEADS)], axis=1)

    lane = lax.broadcasted_iota(I32, (W, W), 1) % ROWS

    def norm_step(t, piece):
        rows, cols = [], []
        for u in range(4):
            i = t * 4 + u
            n = norm_rows(x_ref[i], gain_ref[...], offset_ref[...])
            normed[i] = n
            rows.append(n)
            cols.append(jnp.where(lane == i, wb_rep[...], 0.0).astype(BF))
        return piece + dot(jnp.concatenate(rows, axis=1), jnp.concatenate(cols, axis=0))

    piece = lax.fori_loop(0, ROWS // 4, norm_step, jnp.zeros((W, W), F32))
    plane[core, y] = piece.astype(BF)

    pl.semaphore_wait(barrier, len(greeted))

    y_copies = [
        remote(plane.at[core, y], plane.at[core, y], y_ss.at[n], y_rs.at[n], at_y(s)) for n, s in enumerate(Y_STEPS)
    ]
    for c in y_copies:
        c.start()
    mate_copies = [
        remote(
            normed.at[pl.ds(k * RC, RC)], nbs[k].at[1 + core], n_ss.at[k, 0], n_rs.at[k, 1 + core], mate
        )
        for k in range(CHUNKS)
    ]
    for c in mate_copies:
        c.start()

    def own_step(t, _):
        for u in range(4):
            i = t * 4 + u
            n = normed[i]
            qg = dot_nt(wqg_t[...], n)
            q_t[i] = (qg[:W] * (HD**-0.5 * LOG2E)).astype(BF)
            gate_t[i] = jax.nn.sigmoid(qg[W:] + gb_t[...])
            k_all[i, 0:W] = dot(n, wk_ref[...]).astype(BF)
            v_t[i, :, 0:W] = dot_nt(wv_t[...], n).astype(BF)
        return 0

    lax.fori_loop(0, ROWS // 4, own_step, 0)

    for c in y_copies:
        c.wait_recv()
    cross = remote(plane.at[core], plane.at[core], c_ss, c_rs, mate)
    cross.start()
    side_copies = []
    for k in range(CHUNKS):
        src = normed.at[pl.ds(k * RC, RC)]
        side_copies.append(
            (
                remote(src, nbs[k].at[core], n_ss.at[k, 1], n_rs.at[k, core], at_blk(blk + 2 - core)),
                remote(src, nbs[k].at[2 + core], n_ss.at[k, 2], n_rs.at[k, 2 + core], at_blk(blk - 1 - core)),
            )
        )
        for c in side_copies[-1]:
            c.start()

    remote(plane.at[1 - core], plane.at[1 - core], c_ss, c_rs, mate).wait_recv()

    z_copies = []
    for n, s in enumerate(Z_STEPS):
        there = (z + s + NZ) % NZ
        _, _, _, _, one, two = bias_wants(kept, owner, there * PLANE + y * 2 + core)
        for item, want in enumerate((one, two)):
            local = lax.rem(want + KEPT, PLANE)
            z_send[n, item] = plane[lax.rem(local, 2), local // 2]
        c = remote(z_send.at[n], z_recv.at[z], z_ss.at[n], z_rs.at[n], at_z(s))
        c.start()
        z_copies.append(c)

    diag, g0, g1, g2, one, two = bias_wants(kept, owner, blk)
    for item, want in enumerate((one, two)):
        local = lax.rem(want + KEPT, PLANE)
        z_recv[z, item] = plane[lax.rem(local, 2), local // 2]

    for n, s in enumerate(Z_STEPS):
        remote(z_send.at[n], z_recv.at[(z - s + NZ) % NZ], z_ss.at[n], z_rs.at[n], at_z(s)).wait_recv()

    own = plane[core, y]
    item1 = z_recv[lax.rem(one + KEPT, KEPT) // PLANE, 0]
    item2 = z_recv[lax.rem(two + KEPT, KEPT) // PLANE, 1]
    zero = jnp.zeros_like(own)
    picked[0] = jnp.where(diag, own, item1)
    picked[1] = jnp.where(g1 >= 0, jnp.where(diag, item1, item2), zero)
    picked[2] = jnp.where(g2 >= 0, item2, zero)
    x_copies = [
        remote(picked, whole.at[rep], x_ss.at[n], x_rs.at[n], at_x(s)) for n, s in enumerate(X_STEPS)
    ]
    for c in x_copies:
        c.start()
    whole[rep] = picked[...]

    first, has_first, second, has_second = row_members(kept, blk)
    sel1 = jnp.where(first < 0, 1, 2)
    sel2 = jnp.where(second == -2, 0, jnp.where(second == 1, 2, 3))

    def forward(k):
        remote(normed.at[pl.ds(k * RC, RC)], nbs[k].at[2 * core], n_ss.at[k, 1], n_rs.at[k, 2 * core], mate).wait_recv()
        remote(
            normed.at[pl.ds(k * RC, RC)], nbs[k].at[2 * core + 1], n_ss.at[k, 1], n_rs.at[k, 2 * core + 1], mate
        ).wait_recv()
        c = remote(nbs[k].at[1 + core], nbs[k].at[3 * core], n_ss.at[k, 3], n_rs.at[k, 3 * core], mate)
        c.start()
        return c

    forwards = [forward(0)]

    for n, s in enumerate(X_STEPS):
        remote(picked, whole.at[(rep - s + NX) % NX], x_ss.at[n], x_rs.at[n], at_x(s)).wait_recv()

    group = lax.broadcasted_iota(I32, (W, W), 1) // ROWS
    for t in range(3):
        parts = [whole[r, t].astype(F32) * LOG2E for r in range(NX)]
        if t == 1:
            parts = [jnp.where(has_first, v, MASKED) for v in parts]
        if t == 2:
            parts = [jnp.where(has_second, v, MASKED) for v in parts]
        for h in range(HEADS):
            acc = None
            for r in range(NX):
                shift = ((r - h) * ROWS) % W
                v = pltpu.roll(parts[r], shift, 1) if shift else parts[r]
                acc = v if acc is None else jnp.where(group == r, v, acc)
            bias_t[t * W : (t + 1) * W, h * W : (h + 1) * W] = acc

    row_head = lax.broadcasted_iota(I32, (W, W), 0) // HD

    def score_stage(i, s_ref, m_ref):
        q = q_t[i]
        q_diag = jnp.concatenate(
            [jnp.where(row_head == h, q, jnp.zeros_like(q)) for h in range(HEADS)], axis=1
        )
        s = dot(k_all[i], q_diag) + bias_t[...]
        s_ref[...] = s
        m_ref[...] = jnp.max(s.reshape(48, 8, HEADS * W), axis=0)

    def weight_stage(s_ref, m_ref, p_ref):
        for h in range(HEADS):
            cols = slice(h * W, (h + 1) * W)
            top = jnp.max(m_ref[:, cols], axis=0, keepdims=True)
            p_ref[:, cols] = jnp.exp2(s_ref[:, cols] - top).astype(BF)

    def value_stage(i, p_ref):
        v = v_t[i]
        ones = jnp.ones((16, 3 * W), BF)
        outs = []
        for h in (0, 2):
            r = dot(jnp.concatenate([v[h * HD : (h + 2) * HD], ones], axis=0), p_ref[:, h * W : (h + 2) * W])
            outs.append(r[:HD, :W] * (1.0 / r[2 * HD : 2 * HD + 1, :W]))
            outs.append(r[HD : 2 * HD, W:] * (1.0 / r[2 * HD : 2 * HD + 1, W:]))
        gated[i] = (jnp.concatenate(outs, axis=0) * gate_t[i]).astype(BF)

    ss, ps, ms = (s0, s1), (p0, p1), (m0, m1)

    def step(i, u, score=True, weight=True, value=True):
        if value:
            value_stage(i - 2, ps[u])
        if weight:
            weight_stage(ss[1 - u], ms[1 - u], ps[1 - u])
        if score:
            score_stage(i, ss[u], ms[u])

    def pair_step(t, _):
        step(2 * t, 0)
        step(2 * t + 1, 1)
        return 0

    def out_step(t, _):
        for u in range(4):
            out_ref[t * 4 + u] = dot_tn(gated[t * 4 + u], wo_ref[...]).astype(BF)
        return 0

    for k in range(CHUNKS):
        if k + 1 < CHUNKS:
            forwards.append(forward(k + 1))
        for slot in (2 - core, 3 - 3 * core):
            remote(normed.at[pl.ds(k * RC, RC)], nbs[k].at[slot], n_ss.at[k, 0], n_rs.at[k, slot], mate).wait_recv()

        def key_step(t, _, k=k):
            for u in range(4):
                j = t * 4 + u
                i = k * RC + j
                both = jnp.concatenate([nbs[k][sel1, j], nbs[k][sel2, j]], axis=0)
                k_all[i, W:] = dot(both, wk_ref[...]).astype(BF)
                v_t[i, :, W:] = dot_nt(wv_t[...], both).astype(BF)
            return 0

        lax.fori_loop(0, RC // 4, key_step, 0)
        start = k * RC // 2
        if k == 0:
            step(0, 0, True, False, False)
            step(1, 1, True, True, False)
            start += 1
        lax.fori_loop(start, (k + 1) * RC // 2, pair_step, 0)
        if k:
            lax.fori_loop((k - 1) * RC // 4, k * RC // 4, out_step, 0)
    step(ROWS, 0, False, True, True)
    step(ROWS + 1, 1, False, False, True)
    lax.fori_loop((CHUNKS - 1) * RC // 4, CHUNKS * RC // 4, out_step, 0)

    for c in y_copies + [cross] + z_copies + x_copies + mate_copies + forwards:
        c.wait_send()
    for pair in side_copies:
        for c in pair:
            c.wait_send()


def per_device(
    pair_blocks, kept_pairs, owner, norm_gain, norm_offset, w_query, w_key, w_value, w_gate, gate_bias, w_bias, w_out
):
    vmem = pl.BlockSpec(memory_space=pltpu.VMEM)
    smem = pl.BlockSpec(memory_space=pltpu.SMEM)
    dma = pltpu.SemaphoreType.DMA
    out = pl.pallas_call(
        kernel,
        out_shape=jax.ShapeDtypeStruct((ROWS, W, W), BF),
        in_specs=[smem, smem] + [vmem] * 10,
        out_specs=vmem,
        scratch_shapes=[
            pltpu.VMEM((ROWS, W, W), BF),
            pltpu.VMEM((2, NY, W, W), BF),
            pltpu.VMEM((7, 2, W, W), BF),
            pltpu.VMEM((NZ, 2, W, W), BF),
            pltpu.VMEM((3, W, W), BF),
            pltpu.VMEM((NX, 3, W, W), BF),
        ]
        + [pltpu.VMEM((4, RC, W, W), BF)] * CHUNKS
        + [
            pltpu.VMEM((ROWS, W, W), BF),
            pltpu.VMEM((ROWS, W, W), F32),
            pltpu.VMEM((ROWS, 3 * W, W), BF),
            pltpu.VMEM((ROWS, W, 3 * W), BF),
            pltpu.VMEM((ROWS, W, W), BF),
            pltpu.VMEM((3 * W, HEADS * W), F32),
            pltpu.VMEM((2 * W, W), BF),
            pltpu.VMEM((W, W), BF),
            pltpu.VMEM((W, W), F32),
            pltpu.VMEM((W, W), F32),
        ]
        + [pltpu.VMEM((3 * W, HEADS * W), F32)] * 2
        + [pltpu.VMEM((3 * W, HEADS * W), BF)] * 2
        + [pltpu.VMEM((8, HEADS * W), F32)] * 2
        + [
            dma((7,)), dma((7,)), dma, dma, dma((7,)), dma((7,)), dma((3,)), dma((3,)),
            dma((CHUNKS, 4)), dma((CHUNKS, 4)),
        ],
        compiler_params=pltpu.CompilerParams(
            collective_id=0, has_side_effects=True, vmem_limit_bytes=48 * 2**20
        ),
        name="row_attention",
    )(
        kept_pairs, owner, pair_blocks[0], norm_gain[None], norm_offset[None],
        w_query, w_key, w_value, w_gate, gate_bias[None], w_bias, w_out,
    )
    return out[None]


def solution(mesh):
    return jax.shard_map(
        per_device,
        mesh=mesh,
        in_specs=(P("blk", "rep", None, None),) + (P(),) * 11,
        out_specs=P("blk", "rep", None, None),
        check_vma=False,
    )
```

```python
import functools

import jax
import jax.numpy as jnp
from jax import lax
from jax.experimental import pallas as pl
from jax.experimental.pallas import tpu as pltpu
from jax.sharding import PartitionSpec as P

F32 = jnp.float32
BF = jnp.bfloat16
I32 = jnp.int32
MESH = pl.DeviceIdType.MESH
LOG2E = 1.4426950408889634
MASKED = -1e30

NZ, NY, NX = 8, 8, 4
PLANE = 2 * NY
KEPT = NZ * PLANE
ROWS = 32
W = 128
HEADS, HD = 4, 32
CHUNKS = 4
PARTS = 2
PH = HEADS // PARTS
KL = W // PARTS
RC = ROWS // CHUNKS
STEPS = (1, -1, 2, -2, 3, -3, 4)
X_STEPS = (1, -1, 2)


def dot(a, b):
    return jnp.dot(a, b, preferred_element_type=F32)


def dot_nt(a, b):
    return lax.dot_general(a, b, (((1,), (1,)), ((), ())), preferred_element_type=F32)


def dot_tn(a, b):
    return lax.dot_general(a, b, (((0,), (0,)), ((), ())), preferred_element_type=F32)


def norm_rows(x, gain, offset):
    v = x.astype(F32)
    d = v - jnp.mean(v, axis=-1, keepdims=True)
    s = jnp.mean(d * d, axis=-1, keepdims=True)
    return (d * lax.rsqrt(s + 1e-05) * gain + offset).astype(BF)


def row_members(kept, slot):
    row = kept[0, slot]

    def same(step):
        other = slot + step
        inside = (other >= 0) & (other < KEPT)
        return inside & (kept[0, jnp.clip(other, 0, KEPT - 1)] == row)

    m1, m2, p1, p2 = same(-1), same(-2), same(1), same(2)
    first = jnp.where(m1, -1, 1)
    second = jnp.where(m1 & p1, 1, jnp.where(m2, -2, 2))
    return first, m1 | p1, second, (m1 & p1) | m2 | p2


def bias_wants(kept, owner, slot):
    first, has_first, second, has_second = row_members(kept, slot)
    col = kept[1, slot]
    k1 = kept[1, jnp.clip(slot + first, 0, KEPT - 1)]
    k2 = kept[1, jnp.clip(slot + second, 0, KEPT - 1)]
    g0 = owner[col, col]
    g1 = jnp.where(has_first, owner[col, k1], -1)
    g2 = jnp.where(has_second, owner[col, k2], -1)
    diag = kept[0, slot] == col
    one = jnp.where(diag, g1, g0)
    two = jnp.where(diag, g2, jnp.maximum(g1, g2))
    return diag, g0, g1, g2, one, two


def kernel(
    x_hbm, kept_hbm, owner_hbm, gain_hbm, offset_hbm, wq_hbm, wk_hbm, wv_hbm, wg_hbm, gb_hbm, wb_hbm, wo_hbm,
    out_ref,
    x_ref, kept, owner, gain_ref, offset_ref, wq_ref, wk_ref, wv_ref, wg_ref, gb_ref, wb_ref, wo_ref,
    normed, plane0, plane1, z_send0, z_send1, z_recv0, z_recv1, picked0, picked1, whole0, whole1,
    nb0, nb1, nb2, nb3,
    q_t, gate_t, k_all, v_t, gated, bias0, bias1, wqg_t, wv_t, gb_t, wb_rep,
    s0, s1, p0, p1, m0, m1,
    in_sem, y_ss, y_rs, c_ss, c_rs, z_ss, z_rs, x_ss, x_rs, n_ss, n_rs,
):
    blk = lax.axis_index("blk")
    rep = lax.axis_index("rep")
    z = blk // PLANE
    y = (blk // 2) % NY
    core = blk % 2
    nbs = (nb0, nb1, nb2, nb3)
    planes, z_sends, z_recvs = (plane0, plane1), (z_send0, z_send1), (z_recv0, z_recv1)
    pickeds, wholes, biases = (picked0, picked1), (whole0, whole1), (bias0, bias1)

    def at_blk(b):
        return {"blk": (b + KEPT) % KEPT}

    def at_y(step):
        return {"blk": z * PLANE + ((y + step + NY) % NY) * 2 + core}

    def at_z(step):
        return {"blk": ((z + step + NZ) % NZ) * PLANE + y * 2 + core}

    def at_x(step):
        return {"rep": (rep + step + NX) % NX}

    mate = {"blk": blk + 1 - 2 * core}

    barrier = pltpu.get_barrier_semaphore()
    greeted = [at_y(s) for s in STEPS] + [at_z(s) for s in STEPS] + [at_x(s) for s in X_STEPS] + [mate]
    greeted += [at_blk(blk - 2 + 3 * core), at_blk(blk - 1 + 3 * core)]
    for device in greeted:
        pl.semaphore_signal(barrier, inc=1, device_id=device, device_id_type=MESH)

    operands = (x_hbm, kept_hbm, owner_hbm, gain_hbm, offset_hbm, wq_hbm, wk_hbm, wv_hbm, wg_hbm, gb_hbm, wb_hbm, wo_hbm)
    places = (x_ref, kept, owner, gain_ref, offset_ref, wq_ref, wk_ref, wv_ref, wg_ref, gb_ref, wb_ref, wo_ref)
    fetches = [pltpu.make_async_copy(o, p, in_sem.at[n]) for n, (o, p) in enumerate(zip(operands, places))]
    for c in fetches:
        c.start()
    for c in fetches:
        c.wait()

    def remote(src, dst, ss, rs, device):
        return pltpu.make_async_remote_copy(
            src_ref=src, dst_ref=dst, send_sem=ss, recv_sem=rs, device_id=device, device_id_type=MESH
        )

    def turned(w):
        return w.astype(F32).T.astype(BF)

    wb = jnp.broadcast_to(wb_ref[...].astype(F32)[:, None], (HEADS, ROWS, W)).reshape(W, W)
    wb_rep[...] = wb.T

    lane = lax.broadcasted_iota(I32, (W, W), 1)

    def norm_step(t, piece):
        rows, cols = [], []
        for u in range(4):
            i = t * 4 + u
            n = norm_rows(x_ref[i], gain_ref[...], offset_ref[...])
            normed[i] = n
            rows.append(n)
            cols.append(jnp.where(lane % ROWS == i, wb_rep[...], 0.0).astype(BF))
        return piece + dot(jnp.concatenate(rows, axis=1), jnp.concatenate(cols, axis=0))

    piece = lax.fori_loop(0, ROWS // 4, norm_step, jnp.zeros((W, W), F32))
    span = PH * ROWS
    place = lax.broadcasted_iota(I32, (KL, W), 1) // span
    for p in range(PARTS):
        packed = None
        for hi in range(PARTS):
            v = piece[hi * KL : (hi + 1) * KL]
            shift = ((hi - p) * span) % W
            v = pltpu.roll(v, shift, 1) if shift else v
            packed = v if packed is None else jnp.where(place == hi, v, packed)
        planes[p][core, (y, z)[p]] = packed.astype(BF)

    gather_at, hand_at = (at_y, at_z), (at_z, at_y)
    gather_pos, hand_pos = (y, z), (z, y)

    def gather_index(p, slot):
        slot = lax.rem(slot + KEPT, KEPT)
        return lax.rem(slot // 2, NY) if p == 0 else slot // PLANE

    def hand_index(p, slot):
        return gather_index(1 - p, slot)

    wants = [
        [bias_wants(kept, owner, ((z + s + NZ) % NZ) * PLANE + y * 2 + core)[4:] for s in STEPS],
        [bias_wants(kept, owner, z * PLANE + ((y + s + NY) % NY) * 2 + core)[4:] for s in STEPS],
    ]
    diag, g0, g1, g2, one, two = bias_wants(kept, owner, blk)
    first, has_first, second, has_second = row_members(kept, blk)
    sel1 = jnp.where(first < 0, 1, 2)
    sel2 = jnp.where(second == -2, 0, jnp.where(second == 1, 2, 3))

    pl.semaphore_wait(barrier, len(greeted))

    y_copies = [
        [
            remote(
                planes[p].at[core, gather_pos[p]], planes[p].at[core, gather_pos[p]],
                y_ss.at[p, n], y_rs.at[p, n], gather_at[p](s),
            )
            for n, s in enumerate(STEPS)
        ]
        for p in range(PARTS)
    ]
    sent = []
    for p in range(PARTS):
        for c in y_copies[p]:
            c.start()
            sent.append(c)

    def send_rows(k):
        src = normed.at[pl.ds(k * RC, RC)]
        for c in (
            remote(src, nbs[k].at[core], n_ss.at[k, 1], n_rs.at[k, core], at_blk(blk + 2 - core)),
            remote(src, nbs[k].at[2 + core], n_ss.at[k, 2], n_rs.at[k, 2 + core], at_blk(blk - 1 - core)),
            remote(src, nbs[k].at[1 + core], n_ss.at[k, 0], n_rs.at[k, 1 + core], mate),
        ):
            c.start()
            sent.append(c)

    def cross(p):
        for c in y_copies[p]:
            c.wait_recv()
        c = remote(planes[p].at[core], planes[p].at[core], c_ss.at[p], c_rs.at[p], mate)
        c.start()
        sent.append(c)

    def spread(p):
        remote(planes[p].at[1 - core], planes[p].at[1 - core], c_ss.at[p], c_rs.at[p], mate).wait_recv()
        for n, s in enumerate(STEPS):
            for item, want in enumerate(wants[p][n]):
                z_sends[p][n, item] = planes[p][lax.rem(want + KEPT, 2), gather_index(p, want)]
            c = remote(z_sends[p].at[n], z_recvs[p].at[hand_pos[p]], z_ss.at[p, n], z_rs.at[p, n], hand_at[p](s))
            c.start()
            sent.append(c)
        for item, want in enumerate((one, two)):
            z_recvs[p][hand_pos[p], item] = planes[p][lax.rem(want + KEPT, 2), gather_index(p, want)]

    def pick(p):
        for n, s in enumerate(STEPS):
            there = (hand_pos[p] - s + NZ) % NZ
            remote(z_sends[p].at[n], z_recvs[p].at[there], z_ss.at[p, n], z_rs.at[p, n], hand_at[p](s)).wait_recv()
        own = planes[p][core, gather_pos[p]]
        item1 = z_recvs[p][hand_index(p, one), 0]
        item2 = z_recvs[p][hand_index(p, two), 1]
        zero = jnp.zeros_like(own)
        pickeds[p][0] = jnp.where(diag, own, item1)
        pickeds[p][1] = jnp.where(g1 >= 0, jnp.where(diag, item1, item2), zero)
        pickeds[p][2] = jnp.where(g2 >= 0, item2, zero)
        for n, s in enumerate(X_STEPS):
            c = remote(pickeds[p], wholes[p].at[rep], x_ss.at[p, n], x_rs.at[p, n], at_x(s))
            c.start()
            sent.append(c)
        wholes[p][rep] = pickeds[p][...]

    group = lax.broadcasted_iota(I32, (KL, W), 1) // ROWS

    def lay_out(p):
        for n, s in enumerate(X_STEPS):
            remote(
                pickeds[p], wholes[p].at[(rep - s + NX) % NX], x_ss.at[p, n], x_rs.at[p, n], at_x(s)
            ).wait_recv()
        for t in range(3):
            parts = [wholes[p][r, t].astype(F32) * LOG2E for r in range(NX)]
            if t == 1:
                parts = [jnp.where(has_first, v, MASKED) for v in parts]
            if t == 2:
                parts = [jnp.where(has_second, v, MASKED) for v in parts]
            for hi in range(PARTS):
                for h in range(PH):
                    acc = None
                    for r in range(NX):
                        shift = ((r - hi * PH - h) * ROWS) % W
                        v = pltpu.roll(parts[r], shift, 1) if shift else parts[r]
                        acc = v if acc is None else jnp.where(group == r, v, acc)
                    biases[p][t * W + hi * KL : t * W + (hi + 1) * KL, h * W : (h + 1) * W] = acc

    def own_step(t, _):
        for u in range(4):
            i = t * 4 + u
            n = normed[i]
            qg = dot_nt(wqg_t[...], n)
            q_t[i] = (qg[:W] * (HD**-0.5 * LOG2E)).astype(BF)
            gate_t[i] = jax.nn.sigmoid(qg[W:] + gb_t[...])
            k_all[i, 0:W] = dot(n, wk_ref[...]).astype(BF)
            v_t[i, :, 0:W] = dot_nt(wv_t[...], n).astype(BF)
        return 0

    def rows_ready(k):
        src = normed.at[pl.ds(k * RC, RC)]
        for slot in (2 * core, 2 * core + 1):
            remote(src, nbs[k].at[slot], n_ss.at[k, 1], n_rs.at[k, slot], mate).wait_recv()
        c = remote(nbs[k].at[1 + core], nbs[k].at[3 * core], n_ss.at[k, 3], n_rs.at[k, 3 * core], mate)
        c.start()
        sent.append(c)

    def rows_used(k):
        src = normed.at[pl.ds(k * RC, RC)]
        for slot in (2 - core, 3 - 3 * core):
            remote(src, nbs[k].at[slot], n_ss.at[k, 0], n_rs.at[k, slot], mate).wait_recv()

        def key_step(t, _):
            for u in range(4):
                j = t * 4 + u
                i = k * RC + j
                both = jnp.concatenate([nbs[k][sel1, j], nbs[k][sel2, j]], axis=0)
                k_all[i, W:] = dot(both, wk_ref[...]).astype(BF)
                v_t[i, :, W:] = dot_nt(wv_t[...], both).astype(BF)
            return 0

        lax.fori_loop(0, RC // 4, key_step, 0)

    row_head = lax.broadcasted_iota(I32, (W, W), 0) // HD

    def score_stage(p, rr, s_ref, m_ref):
        for u in range(2):
            q = q_t[rr * 2 + u]
            q_diag = jnp.concatenate(
                [jnp.where(row_head == h, q, jnp.zeros_like(q)) for h in range(p * PH, (p + 1) * PH)], axis=1
            )
            s = dot(k_all[rr * 2 + u], q_diag) + biases[p][...]
            s_ref[u] = s
            m_ref[u] = jnp.max(s.reshape(48, 8, PH * W), axis=0)

    def weight_stage(s_ref, m_ref, p_ref):
        for u in range(2):
            for h in range(PH):
                cols = slice(h * W, (h + 1) * W)
                top = jnp.max(m_ref[u, :, cols], axis=0, keepdims=True)
                p_ref[u, :, cols] = jnp.exp2(s_ref[u, :, cols] - top).astype(BF)

    def value_stage(p, rr, p_ref):
        heads = slice(p * PH * HD, (p + 1) * PH * HD)
        ones = jnp.ones((16, 3 * W), BF)
        for u in range(2):
            i = rr * 2 + u
            r = dot(jnp.concatenate([v_t[i, heads], ones], axis=0), p_ref[u])
            outs = []
            for h in range(PH):
                cols = slice(h * W, (h + 1) * W)
                outs.append(r[h * HD : (h + 1) * HD, cols] * (1.0 / r[PH * HD : PH * HD + 1, cols]))
            gated[i, heads] = (jnp.concatenate(outs, axis=0) * gate_t[i, heads]).astype(BF)

    def step(rr, before=True, here=True):
        if before:
            value_stage(0, rr - 1, p0)
            weight_stage(s1, m1, p1)
        if here:
            score_stage(0, rr, s0, m0)
        if before:
            value_stage(1, rr - 1, p1)
        if here:
            weight_stage(s0, m0, p0)
            score_stage(1, rr, s1, m1)

    def attend(lo, hi):
        def row_step(rr, _):
            step(rr)
            return 0

        if lo == 0:
            step(0, before=False)
        lax.fori_loop(max(lo, 1), hi, row_step, 0)
        if hi == ROWS // 2:
            step(hi, here=False)

    send_rows(0)
    wqg_t[0:W] = turned(wq_ref[...])
    wqg_t[W:] = turned(wg_ref[...])
    cross(0)
    cross(1)
    send_rows(1)
    spread(0)
    spread(1)
    send_rows(2)
    wv_t[...] = turned(wv_ref[...])
    gb_t[...] = jnp.broadcast_to(gb_ref[...], (W, W)).T
    lax.fori_loop(0, ROWS // 4, own_step, 0)
    pick(0)
    pick(1)
    send_rows(3)
    rows_ready(0)
    rows_used(0)
    rows_ready(1)
    lay_out(0)
    lay_out(1)
    for k in range(CHUNKS):
        if k:
            rows_used(k)
        if k and k + 1 < CHUNKS:
            rows_ready(k + 1)
        attend(k * RC // 2, (k + 1) * RC // 2)

    def out_step(t, _):
        for u in range(8):
            out_ref[t * 8 + u] = dot_tn(gated[t * 8 + u], wo_ref[...]).astype(BF)
        return 0

    lax.fori_loop(0, ROWS // 8, out_step, 0)

    for c in sent:
        c.wait_send()


def per_device(
    pair_blocks, kept_pairs, owner, norm_gain, norm_offset, w_query, w_key, w_value, w_gate, gate_bias, w_bias, w_out
):
    hbm = pl.BlockSpec(memory_space=pltpu.HBM)
    dma = pltpu.SemaphoreType.DMA
    operands = (
        pair_blocks[0], kept_pairs.T, owner, norm_gain[None], norm_offset[None],
        w_query, w_key, w_value, w_gate, gate_bias[None], w_bias.T, w_out,
    )
    out = pl.pallas_call(
        kernel,
        out_shape=jax.ShapeDtypeStruct((ROWS, W, W), BF),
        in_specs=[hbm] * len(operands),
        out_specs=pl.BlockSpec(memory_space=pltpu.VMEM),
        scratch_shapes=[
            (pltpu.SMEM if o.dtype == I32 else pltpu.VMEM)(o.shape, o.dtype) for o in operands
        ]
        + [pltpu.VMEM((ROWS, W, W), BF)]
        + [pltpu.VMEM((2, NY, KL, W), BF)] * PARTS
        + [pltpu.VMEM((7, 2, KL, W), BF)] * PARTS
        + [pltpu.VMEM((NZ, 2, KL, W), BF)] * PARTS
        + [pltpu.VMEM((3, KL, W), BF)] * PARTS
        + [pltpu.VMEM((NX, 3, KL, W), BF)] * PARTS
        + [pltpu.VMEM((4, RC, W, W), BF)] * CHUNKS
        + [
            pltpu.VMEM((ROWS, W, W), BF),
            pltpu.VMEM((ROWS, W, W), F32),
            pltpu.VMEM((ROWS, 3 * W, W), BF),
            pltpu.VMEM((ROWS, W, 3 * W), BF),
            pltpu.VMEM((ROWS, W, W), BF),
        ]
        + [pltpu.VMEM((3 * W, PH * W), F32)] * PARTS
        + [
            pltpu.VMEM((2 * W, W), BF),
            pltpu.VMEM((W, W), BF),
            pltpu.VMEM((W, W), F32),
            pltpu.VMEM((W, W), F32),
        ]
        + [pltpu.VMEM((2, 3 * W, PH * W), F32)] * 2
        + [pltpu.VMEM((2, 3 * W, PH * W), BF)] * 2
        + [pltpu.VMEM((2, 8, PH * W), F32)] * 2
        + [
            dma((len(operands),)),
            dma((PARTS, 7)), dma((PARTS, 7)), dma((PARTS,)), dma((PARTS,)), dma((PARTS, 7)), dma((PARTS, 7)),
            dma((PARTS, 3)), dma((PARTS, 3)), dma((CHUNKS, 4)), dma((CHUNKS, 4)),
        ],
        compiler_params=pltpu.CompilerParams(
            collective_id=0, has_side_effects=True, vmem_limit_bytes=40 * 2**20
        ),
        name="row_attention",
    )(*operands)
    return out[None]


def solution(mesh):
    return jax.shard_map(
        per_device,
        mesh=mesh,
        in_specs=(P("blk", "rep", None, None),) + (P(),) * 11,
        out_specs=P("blk", "rep", None, None),
        check_vma=False,
    )
```

```python
import functools

import jax
import jax.numpy as jnp
from jax import lax
from jax.experimental import pallas as pl
from jax.experimental.pallas import tpu as pltpu
from jax.sharding import PartitionSpec as P

F32 = jnp.float32
BF = jnp.bfloat16
I32 = jnp.int32
MESH = pl.DeviceIdType.MESH
LOG2E = 1.4426950408889634
MASKED = -1e30

NZ, NY, NX = 8, 8, 4
PLANE = 2 * NY
KEPT = NZ * PLANE
ROWS = 32
W = 128
HEADS, HD = 4, 32
CHUNKS = 4
PARTS = 2
PH = HEADS // PARTS
KL = W // PARTS
RC = ROWS // CHUNKS
STEPS = (4, 3, -3, 2, -2, 1, -1)
X_STEPS = (2, 1, -1)


def dot(a, b):
    return jnp.dot(a, b, preferred_element_type=F32)


def dot_nt(a, b):
    return lax.dot_general(a, b, (((1,), (1,)), ((), ())), preferred_element_type=F32)


def dot_tn(a, b):
    return lax.dot_general(a, b, (((0,), (0,)), ((), ())), preferred_element_type=F32)


def norm_rows(x, gain, offset):
    v = x.astype(F32)
    d = v - jnp.mean(v, axis=-1, keepdims=True)
    s = jnp.mean(d * d, axis=-1, keepdims=True)
    return (d * lax.rsqrt(s + 1e-05) * gain + offset).astype(BF)


def row_members(kept, slot):
    row = kept[0, slot]

    def same(step):
        other = slot + step
        inside = (other >= 0) & (other < KEPT)
        return inside & (kept[0, jnp.clip(other, 0, KEPT - 1)] == row)

    m1, m2, p1, p2 = same(-1), same(-2), same(1), same(2)
    first = jnp.where(m1, -1, 1)
    second = jnp.where(m1 & p1, 1, jnp.where(m2, -2, 2))
    return first, m1 | p1, second, (m1 & p1) | m2 | p2


def bias_wants(kept, owner, slot):
    first, has_first, second, has_second = row_members(kept, slot)
    col = kept[1, slot]
    k1 = kept[1, jnp.clip(slot + first, 0, KEPT - 1)]
    k2 = kept[1, jnp.clip(slot + second, 0, KEPT - 1)]
    g0 = owner[col, col]
    g1 = jnp.where(has_first, owner[col, k1], -1)
    g2 = jnp.where(has_second, owner[col, k2], -1)
    diag = kept[0, slot] == col
    one = jnp.where(diag, g1, g0)
    two = jnp.where(diag, g2, jnp.maximum(g1, g2))
    return diag, g0, g1, g2, one, two


def kernel(
    x_hbm, kept_hbm, owner_hbm, gain_hbm, offset_hbm, wq_hbm, wk_hbm, wv_hbm, wg_hbm, gb_hbm, wb_hbm, wo_hbm,
    out_ref,
    x_ref, kept, owner, gain_ref, offset_ref, wq_ref, wk_ref, wv_ref, wg_ref, gb_ref, wb_ref, wo_ref,
    normed, plane0, plane1, z_send0, z_send1, z_recv0, z_recv1, picked0, picked1, whole0, whole1,
    nb0, nb1, nb2, nb3,
    q_t, gate_t, k_all, v_t, gated, bias0, bias1, wqg_t, wv_t, gb_t, wb_rep,
    s0, s1, p0, p1, m0, m1,
    in_sem, y_ss, y_rs, c_ss, c_rs, z_ss, z_rs, x_ss, x_rs, n_ss, n_rs,
):
    blk = lax.axis_index("blk")
    rep = lax.axis_index("rep")
    z = blk // PLANE
    y = (blk // 2) % NY
    core = blk % 2
    nbs = (nb0, nb1, nb2, nb3)
    planes, z_sends, z_recvs = (plane0, plane1), (z_send0, z_send1), (z_recv0, z_recv1)
    pickeds, wholes, biases = (picked0, picked1), (whole0, whole1), (bias0, bias1)

    def at_blk(b):
        return {"blk": (b + KEPT) % KEPT}

    def at_y(step):
        return {"blk": z * PLANE + ((y + step + NY) % NY) * 2 + core}

    def at_z(step):
        return {"blk": ((z + step + NZ) % NZ) * PLANE + y * 2 + core}

    def at_x(step):
        return {"rep": (rep + step + NX) % NX}

    mate = {"blk": blk + 1 - 2 * core}

    barrier = pltpu.get_barrier_semaphore()
    greeted = [at_y(s) for s in STEPS] + [at_z(s) for s in STEPS] + [at_x(s) for s in X_STEPS] + [mate]
    greeted += [at_blk(blk - 2), at_blk(blk + 2)]
    for device in greeted:
        pl.semaphore_signal(barrier, inc=1, device_id=device, device_id_type=MESH)

    operands = (x_hbm, kept_hbm, owner_hbm, gain_hbm, offset_hbm, wq_hbm, wk_hbm, wv_hbm, wg_hbm, gb_hbm, wb_hbm, wo_hbm)
    places = (x_ref, kept, owner, gain_ref, offset_ref, wq_ref, wk_ref, wv_ref, wg_ref, gb_ref, wb_ref, wo_ref)
    fetches = [pltpu.make_async_copy(o, p, in_sem.at[n]) for n, (o, p) in enumerate(zip(operands, places))]
    for c in fetches:
        c.start()
    for n in (0, 3, 4, 10):
        fetches[n].wait()

    def remote(src, dst, ss, rs, device):
        return pltpu.make_async_remote_copy(
            src_ref=src, dst_ref=dst, send_sem=ss, recv_sem=rs, device_id=device, device_id_type=MESH
        )

    def turned(w):
        return w.astype(F32).T.astype(BF)

    wb = jnp.broadcast_to(wb_ref[...].astype(F32)[:, None], (HEADS, ROWS, W)).reshape(W, W)
    wb_rep[...] = wb.T

    lane = lax.broadcasted_iota(I32, (W, W), 1)

    def norm_step(t, piece):
        rows, cols = [], []
        for u in range(4):
            i = t * 4 + u
            n = norm_rows(x_ref[i], gain_ref[...], offset_ref[...])
            normed[i] = n
            rows.append(n)
            cols.append(jnp.where(lane % ROWS == i, wb_rep[...], 0.0).astype(BF))
        return piece + dot(jnp.concatenate(rows, axis=1), jnp.concatenate(cols, axis=0))

    sent = []

    def send_rows(k):
        src = normed.at[pl.ds(k * RC, RC)]
        for c in (
            remote(src, nbs[k].at[0], n_ss.at[k, 1], n_rs.at[k, 0], at_blk(blk + 2)),
            remote(src, nbs[k].at[3], n_ss.at[k, 2], n_rs.at[k, 3], at_blk(blk - 2)),
            remote(src, nbs[k].at[1 + core], n_ss.at[k, 0], n_rs.at[k, 1 + core], mate),
        ):
            c.start()
            sent.append(c)

    piece = lax.fori_loop(0, ROWS // 4, norm_step, jnp.zeros((W, W), F32))
    span = PH * ROWS
    place = lax.broadcasted_iota(I32, (KL, W), 1) // span
    for p in range(PARTS):
        packed = None
        for hi in range(PARTS):
            v = piece[hi * KL : (hi + 1) * KL]
            shift = ((hi - p) * span) % W
            v = pltpu.roll(v, shift, 1) if shift else v
            packed = v if packed is None else jnp.where(place == hi, v, packed)
        planes[p][core, (y, z)[p]] = packed.astype(BF)

    gather_at, hand_at = (at_y, at_z), (at_z, at_y)
    gather_pos, hand_pos = (y, z), (z, y)

    def gather_index(p, slot):
        slot = lax.rem(slot + KEPT, KEPT)
        return lax.rem(slot // 2, NY) if p == 0 else slot // PLANE

    def hand_index(p, slot):
        return gather_index(1 - p, slot)

    pl.semaphore_wait(barrier, len(greeted))

    y_copies = [
        [
            remote(
                planes[p].at[core, gather_pos[p]], planes[p].at[core, gather_pos[p]],
                y_ss.at[p, n], y_rs.at[p, n], gather_at[p](s),
            )
            for n, s in enumerate(STEPS)
        ]
        for p in range(PARTS)
    ]
    for p in range(PARTS):
        for c in y_copies[p]:
            c.start()
            sent.append(c)

    for n in (1, 2, 5, 6, 7, 8, 9, 11):
        fetches[n].wait()
    wants = [
        [bias_wants(kept, owner, ((z + s + NZ) % NZ) * PLANE + y * 2 + core)[4:] for s in STEPS],
        [bias_wants(kept, owner, z * PLANE + ((y + s + NY) % NY) * 2 + core)[4:] for s in STEPS],
    ]
    diag, g0, g1, g2, one, two = bias_wants(kept, owner, blk)
    first, has_first, second, has_second = row_members(kept, blk)
    sel1 = jnp.where(first < 0, 1, 2)
    sel2 = jnp.where(second == -2, 0, jnp.where(second == 1, 2, 3))

    def cross(p):
        for c in y_copies[p]:
            c.wait_recv()
        c = remote(planes[p].at[core], planes[p].at[core], c_ss.at[p], c_rs.at[p], mate)
        c.start()
        sent.append(c)

    def spread(p):
        remote(planes[p].at[1 - core], planes[p].at[1 - core], c_ss.at[p], c_rs.at[p], mate).wait_recv()
        for n, s in enumerate(STEPS):
            for item, want in enumerate(wants[p][n]):
                z_sends[p][n, item] = planes[p][lax.rem(want + KEPT, 2), gather_index(p, want)]
            c = remote(z_sends[p].at[n], z_recvs[p].at[hand_pos[p]], z_ss.at[p, n], z_rs.at[p, n], hand_at[p](s))
            c.start()
            sent.append(c)
        for item, want in enumerate((one, two)):
            z_recvs[p][hand_pos[p], item] = planes[p][lax.rem(want + KEPT, 2), gather_index(p, want)]

    def pick(p):
        for n, s in enumerate(STEPS):
            there = (hand_pos[p] - s + NZ) % NZ
            remote(z_sends[p].at[n], z_recvs[p].at[there], z_ss.at[p, n], z_rs.at[p, n], hand_at[p](s)).wait_recv()
        own = planes[p][core, gather_pos[p]]
        item1 = z_recvs[p][hand_index(p, one), 0]
        item2 = z_recvs[p][hand_index(p, two), 1]
        zero = jnp.zeros_like(own)
        pickeds[p][0] = jnp.where(diag, own, item1)
        pickeds[p][1] = jnp.where(g1 >= 0, jnp.where(diag, item1, item2), zero)
        pickeds[p][2] = jnp.where(g2 >= 0, item2, zero)
        for n, s in enumerate(X_STEPS):
            c = remote(pickeds[p], wholes[p].at[rep], x_ss.at[p, n], x_rs.at[p, n], at_x(s))
            c.start()
            sent.append(c)
        wholes[p][rep] = pickeds[p][...]

    group = lax.broadcasted_iota(I32, (KL, W), 1) // ROWS

    def lay_out(p):
        for n, s in enumerate(X_STEPS):
            remote(
                pickeds[p], wholes[p].at[(rep - s + NX) % NX], x_ss.at[p, n], x_rs.at[p, n], at_x(s)
            ).wait_recv()
        for t in range(3):
            parts = [wholes[p][r, t].astype(F32) * LOG2E for r in range(NX)]
            if t == 1:
                parts = [jnp.where(has_first, v, MASKED) for v in parts]
            if t == 2:
                parts = [jnp.where(has_second, v, MASKED) for v in parts]
            for hi in range(PARTS):
                for h in range(PH):
                    acc = None
                    for r in range(NX):
                        shift = ((r - hi * PH - h) * ROWS) % W
                        v = pltpu.roll(parts[r], shift, 1) if shift else parts[r]
                        acc = v if acc is None else jnp.where(group == r, v, acc)
                    biases[p][t * W + hi * KL : t * W + (hi + 1) * KL, h * W : (h + 1) * W] = acc

    def own_step(t, _):
        for u in range(4):
            i = t * 4 + u
            n = normed[i]
            qg = dot_nt(wqg_t[...], n)
            q_t[i] = (qg[:W] * (HD**-0.5 * LOG2E)).astype(BF)
            gate_t[i] = jax.nn.sigmoid(qg[W:] + gb_t[...])
            k_all[i, 0:W] = dot(n, wk_ref[...]).astype(BF)
            v_t[i, :, 0:W] = dot_nt(wv_t[...], n).astype(BF)
        return 0

    def rows_ready(k):
        src = normed.at[pl.ds(k * RC, RC)]
        for slot in (0, 3):
            remote(src, nbs[k].at[slot], n_ss.at[k, 1], n_rs.at[k, slot], mate).wait_recv()
        c = remote(nbs[k].at[3 - 3 * core], nbs[k].at[2 - core], n_ss.at[k, 3], n_rs.at[k, 2 - core], mate)
        c.start()
        sent.append(c)

    def rows_used(k):
        src = normed.at[pl.ds(k * RC, RC)]
        for slot in (2 - core, 1 + core):
            remote(src, nbs[k].at[slot], n_ss.at[k, 0], n_rs.at[k, slot], mate).wait_recv()

        def key_step(t, _):
            for u in range(4):
                j = t * 4 + u
                i = k * RC + j
                both = jnp.concatenate([nbs[k][sel1, j], nbs[k][sel2, j]], axis=0)
                k_all[i, W:] = dot(both, wk_ref[...]).astype(BF)
                v_t[i, :, W:] = dot_nt(wv_t[...], both).astype(BF)
            return 0

        lax.fori_loop(0, RC // 4, key_step, 0)

    row_head = lax.broadcasted_iota(I32, (W, W), 0) // HD

    def score_stage(p, rr, s_ref, m_ref):
        for u in range(2):
            q = q_t[rr * 2 + u]
            q_diag = jnp.concatenate(
                [jnp.where(row_head == h, q, jnp.zeros_like(q)) for h in range(p * PH, (p + 1) * PH)], axis=1
            )
            s = dot(k_all[rr * 2 + u], q_diag) + biases[p][...]
            s_ref[u] = s
            m_ref[u] = jnp.max(s.reshape(48, 8, PH * W), axis=0)

    def weight_stage(s_ref, m_ref, p_ref):
        for u in range(2):
            for h in range(PH):
                cols = slice(h * W, (h + 1) * W)
                top = jnp.max(m_ref[u, :, cols], axis=0, keepdims=True)
                p_ref[u, :, cols] = jnp.exp2(s_ref[u, :, cols] - top).astype(BF)

    def value_stage(p, rr, p_ref):
        heads = slice(p * PH * HD, (p + 1) * PH * HD)
        ones = jnp.ones((16, 3 * W), BF)
        for u in range(2):
            i = rr * 2 + u
            r = dot(jnp.concatenate([v_t[i, heads], ones], axis=0), p_ref[u])
            outs = []
            for h in range(PH):
                cols = slice(h * W, (h + 1) * W)
                outs.append(r[h * HD : (h + 1) * HD, cols] * (1.0 / r[PH * HD : PH * HD + 1, cols]))
            gated[i, heads] = (jnp.concatenate(outs, axis=0) * gate_t[i, heads]).astype(BF)

    def step(rr, before=True, here=True):
        if before:
            value_stage(0, rr - 1, p0)
            weight_stage(s1, m1, p1)
        if here:
            score_stage(0, rr, s0, m0)
        if before:
            value_stage(1, rr - 1, p1)
        if here:
            weight_stage(s0, m0, p0)
            score_stage(1, rr, s1, m1)

    def attend(lo, hi):
        def row_step(rr, _):
            step(rr)
            return 0

        if lo == 0:
            step(0, before=False)
        lax.fori_loop(max(lo, 1), hi, row_step, 0)
        if hi == ROWS // 2:
            step(hi, here=False)

    def out_step(t, _):
        for u in range(RC):
            out_ref[t * RC + u] = dot_tn(gated[t * RC + u], wo_ref[...]).astype(BF)
        return 0

    wqg_t[0:W] = turned(wq_ref[...])
    wqg_t[W:] = turned(wg_ref[...])
    cross(0)
    cross(1)
    send_rows(0)
    spread(0)
    spread(1)
    send_rows(1)
    wv_t[...] = turned(wv_ref[...])
    gb_t[...] = jnp.broadcast_to(gb_ref[...], (W, W)).T
    lax.fori_loop(0, ROWS // 4, own_step, 0)
    send_rows(2)
    send_rows(3)
    pick(0)
    pick(1)
    rows_ready(0)
    rows_used(0)
    rows_ready(1)
    lay_out(0)
    lay_out(1)
    for k in range(CHUNKS):
        if k:
            rows_used(k)
        if k and k + 1 < CHUNKS:
            rows_ready(k + 1)
        attend(k * RC // 2, (k + 1) * RC // 2)
        if k:
            lax.fori_loop(k - 1, k, out_step, 0)
    lax.fori_loop(CHUNKS - 1, CHUNKS, out_step, 0)

    for c in sent:
        c.wait_send()


def per_device(
    pair_blocks, kept_pairs, owner, norm_gain, norm_offset, w_query, w_key, w_value, w_gate, gate_bias, w_bias, w_out
):
    hbm = pl.BlockSpec(memory_space=pltpu.HBM)
    dma = pltpu.SemaphoreType.DMA
    operands = (
        pair_blocks[0], kept_pairs.T, owner, norm_gain[None], norm_offset[None],
        w_query, w_key, w_value, w_gate, gate_bias[None], w_bias.T, w_out,
    )
    out = pl.pallas_call(
        kernel,
        out_shape=jax.ShapeDtypeStruct((ROWS, W, W), BF),
        in_specs=[hbm] * len(operands),
        out_specs=pl.BlockSpec(memory_space=pltpu.VMEM),
        scratch_shapes=[
            (pltpu.SMEM if o.dtype == I32 else pltpu.VMEM)(o.shape, o.dtype) for o in operands
        ]
        + [pltpu.VMEM((ROWS, W, W), BF)]
        + [pltpu.VMEM((2, NY, KL, W), BF)] * PARTS
        + [pltpu.VMEM((7, 2, KL, W), BF)] * PARTS
        + [pltpu.VMEM((NZ, 2, KL, W), BF)] * PARTS
        + [pltpu.VMEM((3, KL, W), BF)] * PARTS
        + [pltpu.VMEM((NX, 3, KL, W), BF)] * PARTS
        + [pltpu.VMEM((4, RC, W, W), BF)] * CHUNKS
        + [
            pltpu.VMEM((ROWS, W, W), BF),
            pltpu.VMEM((ROWS, W, W), F32),
            pltpu.VMEM((ROWS, 3 * W, W), BF),
            pltpu.VMEM((ROWS, W, 3 * W), BF),
            pltpu.VMEM((ROWS, W, W), BF),
        ]
        + [pltpu.VMEM((3 * W, PH * W), F32)] * PARTS
        + [
            pltpu.VMEM((2 * W, W), BF),
            pltpu.VMEM((W, W), BF),
            pltpu.VMEM((W, W), F32),
            pltpu.VMEM((W, W), F32),
        ]
        + [pltpu.VMEM((2, 3 * W, PH * W), F32)] * 2
        + [pltpu.VMEM((2, 3 * W, PH * W), BF)] * 2
        + [pltpu.VMEM((2, 8, PH * W), F32)] * 2
        + [
            dma((len(operands),)),
            dma((PARTS, 7)), dma((PARTS, 7)), dma((PARTS,)), dma((PARTS,)), dma((PARTS, 7)), dma((PARTS, 7)),
            dma((PARTS, 3)), dma((PARTS, 3)), dma((CHUNKS, 4)), dma((CHUNKS, 4)),
        ],
        compiler_params=pltpu.CompilerParams(
            collective_id=0, has_side_effects=True, vmem_limit_bytes=60 * 2**20
        ),
        name="row_attention",
    )(*operands)
    return out[None]


def solution(mesh):
    return jax.shard_map(
        per_device,
        mesh=mesh,
        in_specs=(P("blk", "rep", None, None),) + (P(),) * 11,
        out_specs=P("blk", "rep", None, None),
        check_vma=False,
    )
```

```python
import functools

import jax
import jax.numpy as jnp
from jax import lax
from jax.experimental import pallas as pl
from jax.experimental.pallas import tpu as pltpu
from jax.sharding import PartitionSpec as P

F32 = jnp.float32
BF = jnp.bfloat16
I32 = jnp.int32
MESH = pl.DeviceIdType.MESH
LOG2E = 1.4426950408889634
MASKED = -1e30

NZ, NY, NX = 8, 8, 4
PLANE = 2 * NY
KEPT = NZ * PLANE
ROWS = 32
W = 128
HEADS, HD = 4, 32
CHUNKS = 8
PARTS = 2
PH = HEADS // PARTS
KL = W // PARTS
RC = ROWS // CHUNKS
STEPS = (4, 3, -3, 2, -2, 1, -1)
X_STEPS = (2, 1, -1)


def dot(a, b):
    return jnp.dot(a, b, preferred_element_type=F32)


def dot_nt(a, b):
    return lax.dot_general(a, b, (((1,), (1,)), ((), ())), preferred_element_type=F32)


def dot_tn(a, b):
    return lax.dot_general(a, b, (((0,), (0,)), ((), ())), preferred_element_type=F32)


def norm_rows(x, gain, offset):
    v = x.astype(F32)
    d = v - jnp.mean(v, axis=-1, keepdims=True)
    s = jnp.mean(d * d, axis=-1, keepdims=True)
    return (d * lax.rsqrt(s + 1e-05) * gain + offset).astype(BF)


def row_members(kept, slot):
    row = kept[0, slot]

    def same(step):
        other = slot + step
        inside = (other >= 0) & (other < KEPT)
        return inside & (kept[0, jnp.clip(other, 0, KEPT - 1)] == row)

    m1, m2, p1, p2 = same(-1), same(-2), same(1), same(2)
    first = jnp.where(m1, -1, 1)
    second = jnp.where(m1 & p1, 1, jnp.where(m2, -2, 2))
    return first, m1 | p1, second, (m1 & p1) | m2 | p2


def bias_wants(kept, owner, slot):
    first, has_first, second, has_second = row_members(kept, slot)
    col = kept[1, slot]
    k1 = kept[1, jnp.clip(slot + first, 0, KEPT - 1)]
    k2 = kept[1, jnp.clip(slot + second, 0, KEPT - 1)]
    g0 = owner[col, col]
    g1 = jnp.where(has_first, owner[col, k1], -1)
    g2 = jnp.where(has_second, owner[col, k2], -1)
    diag = kept[0, slot] == col
    one = jnp.where(diag, g1, g0)
    two = jnp.where(diag, g2, jnp.maximum(g1, g2))
    return diag, g0, g1, g2, one, two


def kernel(
    x_hbm, kept_hbm, owner_hbm, gain_hbm, offset_hbm, wq_hbm, wk_hbm, wv_hbm, wg_hbm, gb_hbm, wb_hbm, wo_hbm,
    out_hbm,
    x_ref, kept, owner, gain_ref, offset_ref, wq_ref, wk_ref, wv_ref, wg_ref, gb_ref, wb_ref, wo_ref,
    normed, plane0, plane1, z_send0, z_send1, z_recv0, z_recv1, picked0, picked1, whole0, whole1,
    own_piece, whole_own, q_t, gate_t, k_all, v_t, gated, out_ref, bias0, bias1, wqg_t, wv_t, gb_t, wb_rep,
    s0, s1, p0, p1, m0, m1,
    in_sem, out_sem, y_ss, y_rs, c_ss, c_rs, z_ss, z_rs, o_ss, o_rs, x_ss, x_rs, n_ss, n_rs, *nbs
):
    blk = lax.axis_index("blk")
    rep = lax.axis_index("rep")
    z = blk // PLANE
    y = (blk // 2) % NY
    core = blk % 2
    planes, z_sends, z_recvs = (plane0, plane1), (z_send0, z_send1), (z_recv0, z_recv1)
    pickeds, wholes, biases = (picked0, picked1), (whole0, whole1), (bias0, bias1)

    def at_blk(b):
        return {"blk": (b + KEPT) % KEPT}

    def at_y(step):
        return {"blk": z * PLANE + ((y + step + NY) % NY) * 2 + core}

    def at_z(step):
        return {"blk": ((z + step + NZ) % NZ) * PLANE + y * 2 + core}

    def at_x(step):
        return {"rep": (rep + step + NX) % NX}

    mate = {"blk": blk + 1 - 2 * core}

    barrier = pltpu.get_barrier_semaphore()
    greeted = [at_y(s) for s in STEPS] + [at_z(s) for s in STEPS] + [at_x(s) for s in X_STEPS] + [mate]
    greeted += [at_blk(blk - 2), at_blk(blk + 2)]
    for device in greeted:
        pl.semaphore_signal(barrier, inc=1, device_id=device, device_id_type=MESH)

    operands = (x_hbm, kept_hbm, owner_hbm, gain_hbm, offset_hbm, wq_hbm, wk_hbm, wv_hbm, wg_hbm, gb_hbm, wb_hbm, wo_hbm)
    places = (x_ref, kept, owner, gain_ref, offset_ref, wq_ref, wk_ref, wv_ref, wg_ref, gb_ref, wb_ref, wo_ref)
    fetches = [pltpu.make_async_copy(o, p, in_sem.at[n]) for n, (o, p) in enumerate(zip(operands, places))]
    for c in fetches:
        c.start()
    for n in (0, 3, 4, 10):
        fetches[n].wait()

    def remote(src, dst, ss, rs, device):
        return pltpu.make_async_remote_copy(
            src_ref=src, dst_ref=dst, send_sem=ss, recv_sem=rs, device_id=device, device_id_type=MESH
        )

    def turned(w):
        return w.astype(F32).T.astype(BF)

    wb = jnp.broadcast_to(wb_ref[...].astype(F32)[:, None], (HEADS, ROWS, W)).reshape(W, W)
    wb_rep[...] = wb.T

    lane = lax.broadcasted_iota(I32, (W, W), 1)

    def norm_step(t, piece):
        rows, cols = [], []
        for u in range(4):
            i = t * 4 + u
            n = norm_rows(x_ref[i], gain_ref[...], offset_ref[...])
            normed[i] = n
            rows.append(n)
            cols.append(jnp.where(lane % ROWS == i, wb_rep[...], 0.0).astype(BF))
        return piece + dot(jnp.concatenate(rows, axis=1), jnp.concatenate(cols, axis=0))

    sent = []

    def send_rows(k):
        src = normed.at[pl.ds(k * RC, RC)]
        for c in (
            remote(src, nbs[k].at[0], n_ss.at[k, 1], n_rs.at[k, 0], at_blk(blk + 2)),
            remote(src, nbs[k].at[3], n_ss.at[k, 2], n_rs.at[k, 3], at_blk(blk - 2)),
            remote(src, nbs[k].at[1 + core], n_ss.at[k, 0], n_rs.at[k, 1 + core], mate),
        ):
            c.start()
            sent.append(c)

    piece = lax.fori_loop(0, ROWS // 4, norm_step, jnp.zeros((W, W), F32))
    span = PH * ROWS
    place = lax.broadcasted_iota(I32, (KL, W), 1) // span
    for p in range(PARTS):
        packed = None
        for hi in range(PARTS):
            v = piece[hi * KL : (hi + 1) * KL]
            shift = ((hi - p) * span) % W
            v = pltpu.roll(v, shift, 1) if shift else v
            packed = v if packed is None else jnp.where(place == hi, v, packed)
        own_piece[p] = packed.astype(BF)
        planes[p][core, (y, z)[p]] = packed.astype(BF)

    gather_at, hand_at = (at_y, at_z), (at_z, at_y)
    gather_pos, hand_pos = (y, z), (z, y)

    def gather_index(p, slot):
        slot = lax.rem(slot + KEPT, KEPT)
        return lax.rem(slot // 2, NY) if p == 0 else slot // PLANE

    def hand_index(p, slot):
        return gather_index(1 - p, slot)

    pl.semaphore_wait(barrier, len(greeted))

    y_copies = [
        [
            remote(
                planes[p].at[core, gather_pos[p]], planes[p].at[core, gather_pos[p]],
                y_ss.at[p, n], y_rs.at[p, n], gather_at[p](s),
            )
            for n, s in enumerate(STEPS)
        ]
        for p in range(PARTS)
    ]
    for p in range(PARTS):
        for c in y_copies[p]:
            c.start()
            sent.append(c)
    for n, s in enumerate(X_STEPS):
        c = remote(own_piece, whole_own.at[rep], o_ss.at[n], o_rs.at[n], at_x(s))
        c.start()
        sent.append(c)
    whole_own[rep] = own_piece[...]

    for n in (1, 2, 5, 6, 7, 8, 9, 11):
        fetches[n].wait()
    wants = [
        [bias_wants(kept, owner, ((z + s + NZ) % NZ) * PLANE + y * 2 + core)[4:] for s in STEPS],
        [bias_wants(kept, owner, z * PLANE + ((y + s + NY) % NY) * 2 + core)[4:] for s in STEPS],
    ]
    diag, g0, g1, g2, one, two = bias_wants(kept, owner, blk)
    first, has_first, second, has_second = row_members(kept, blk)
    sel1 = jnp.where(first < 0, 1, 2)
    sel2 = jnp.where(second == -2, 0, jnp.where(second == 1, 2, 3))

    def cross(p):
        for c in y_copies[p]:
            c.wait_recv()
        c = remote(planes[p].at[core], planes[p].at[core], c_ss.at[p], c_rs.at[p], mate)
        c.start()
        sent.append(c)

    def spread(p):
        remote(planes[p].at[1 - core], planes[p].at[1 - core], c_ss.at[p], c_rs.at[p], mate).wait_recv()
        for n, s in enumerate(STEPS):
            for item, want in enumerate(wants[p][n]):
                z_sends[p][n, item] = planes[p][lax.rem(want + KEPT, 2), gather_index(p, want)]
            c = remote(z_sends[p].at[n], z_recvs[p].at[hand_pos[p]], z_ss.at[p, n], z_rs.at[p, n], hand_at[p](s))
            c.start()
            sent.append(c)
        for item, want in enumerate((one, two)):
            z_recvs[p][hand_pos[p], item] = planes[p][lax.rem(want + KEPT, 2), gather_index(p, want)]

    def pick(p):
        for n, s in enumerate(STEPS):
            there = (hand_pos[p] - s + NZ) % NZ
            remote(z_sends[p].at[n], z_recvs[p].at[there], z_ss.at[p, n], z_rs.at[p, n], hand_at[p](s)).wait_recv()
        pickeds[p][0] = z_recvs[p][hand_index(p, one), 0]
        pickeds[p][1] = z_recvs[p][hand_index(p, two), 1]
        for n, s in enumerate(X_STEPS):
            c = remote(pickeds[p], wholes[p].at[rep], x_ss.at[p, n], x_rs.at[p, n], at_x(s))
            c.start()
            sent.append(c)
        wholes[p][rep] = pickeds[p][...]

    group = lax.broadcasted_iota(I32, (KL, W), 1) // ROWS

    def lay_out(p):
        if p == 0:
            for n, s in enumerate(X_STEPS):
                remote(own_piece, whole_own.at[(rep - s + NX) % NX], o_ss.at[n], o_rs.at[n], at_x(s)).wait_recv()
        for n, s in enumerate(X_STEPS):
            remote(
                pickeds[p], wholes[p].at[(rep - s + NX) % NX], x_ss.at[p, n], x_rs.at[p, n], at_x(s)
            ).wait_recv()
        owns = [whole_own[r, p].astype(F32) * LOG2E for r in range(NX)]
        ones = [wholes[p][r, 0].astype(F32) * LOG2E for r in range(NX)]
        twos = [wholes[p][r, 1].astype(F32) * LOG2E for r in range(NX)]
        for t in range(3):
            if t == 0:
                parts = [jnp.where(diag, a, b) for a, b in zip(owns, ones)]
            if t == 1:
                blank = jnp.where(has_first, 0.0, MASKED)
                parts = [jnp.where(g1 >= 0, jnp.where(diag, a, b), blank) for a, b in zip(ones, twos)]
            if t == 2:
                blank = jnp.where(has_second, 0.0, MASKED)
                parts = [jnp.where(g2 >= 0, b, blank) for b in twos]
            for hi in range(PARTS):
                for h in range(PH):
                    acc = None
                    for r in range(NX):
                        shift = ((r - hi * PH - h) * ROWS) % W
                        v = pltpu.roll(parts[r], shift, 1) if shift else parts[r]
                        acc = v if acc is None else jnp.where(group == r, v, acc)
                    biases[p][t * W + hi * KL : t * W + (hi + 1) * KL, h * W : (h + 1) * W] = acc

    def own_step(t, _):
        for u in range(4):
            i = t * 4 + u
            n = normed[i]
            qg = dot_nt(wqg_t[...], n)
            q_t[i] = (qg[:W] * (HD**-0.5 * LOG2E)).astype(BF)
            gate_t[i] = jax.nn.sigmoid(qg[W:] + gb_t[...])
            k_all[i, 0:W] = dot(n, wk_ref[...]).astype(BF)
            v_t[i, :, 0:W] = dot_nt(wv_t[...], n).astype(BF)
        return 0

    def rows_ready(k):
        src = normed.at[pl.ds(k * RC, RC)]
        for slot in (0, 3):
            remote(src, nbs[k].at[slot], n_ss.at[k, 1], n_rs.at[k, slot], mate).wait_recv()
        c = remote(nbs[k].at[3 - 3 * core], nbs[k].at[2 - core], n_ss.at[k, 3], n_rs.at[k, 2 - core], mate)
        c.start()
        sent.append(c)

    def rows_used(k):
        src = normed.at[pl.ds(k * RC, RC)]
        for slot in (2 - core, 1 + core):
            remote(src, nbs[k].at[slot], n_ss.at[k, 0], n_rs.at[k, slot], mate).wait_recv()

        def key_step(t, _):
            for u in range(4):
                j = t * 4 + u
                i = k * RC + j
                both = jnp.concatenate([nbs[k][sel1, j], nbs[k][sel2, j]], axis=0)
                k_all[i, W:] = dot(both, wk_ref[...]).astype(BF)
                v_t[i, :, W:] = dot_nt(wv_t[...], both).astype(BF)
            return 0

        lax.fori_loop(0, RC // 4, key_step, 0)

    row_head = lax.broadcasted_iota(I32, (W, W), 0) // HD

    def score_stage(p, rr, s_ref, m_ref):
        for u in range(2):
            q = q_t[rr * 2 + u]
            q_diag = jnp.concatenate(
                [jnp.where(row_head == h, q, jnp.zeros_like(q)) for h in range(p * PH, (p + 1) * PH)], axis=1
            )
            s = dot(k_all[rr * 2 + u], q_diag) + biases[p][...]
            s_ref[u] = s
            m_ref[u] = jnp.max(s.reshape(48, 8, PH * W), axis=0)

    def weight_stage(s_ref, m_ref, p_ref):
        for u in range(2):
            for h in range(PH):
                cols = slice(h * W, (h + 1) * W)
                top = jnp.max(m_ref[u, :, cols], axis=0, keepdims=True)
                p_ref[u, :, cols] = jnp.exp2(s_ref[u, :, cols] - top).astype(BF)

    def value_stage(p, rr, p_ref):
        heads = slice(p * PH * HD, (p + 1) * PH * HD)
        ones = jnp.ones((16, 3 * W), BF)
        for u in range(2):
            i = rr * 2 + u
            r = dot(jnp.concatenate([v_t[i, heads], ones], axis=0), p_ref[u])
            outs = []
            for h in range(PH):
                cols = slice(h * W, (h + 1) * W)
                outs.append(r[h * HD : (h + 1) * HD, cols] * (1.0 / r[PH * HD : PH * HD + 1, cols]))
            gated[i, heads] = (jnp.concatenate(outs, axis=0) * gate_t[i, heads]).astype(BF)

    def step(rr, before=True, here=True):
        if before:
            value_stage(0, rr - 1, p0)
            weight_stage(s1, m1, p1)
        if here:
            score_stage(0, rr, s0, m0)
        if before:
            value_stage(1, rr - 1, p1)
        if here:
            weight_stage(s0, m0, p0)
            score_stage(1, rr, s1, m1)

    def attend(lo, hi):
        def row_step(rr, _):
            step(rr)
            return 0

        if lo == 0:
            step(0, before=False)
        lax.fori_loop(max(lo, 1), hi, row_step, 0)
        if hi == ROWS // 2:
            step(hi, here=False)

    def write(k):
        for i in range(k * RC, (k + 1) * RC):
            out_ref[i] = dot_tn(gated[i], wo_ref[...]).astype(BF)
        rows = pl.ds(k * RC, RC)
        c = pltpu.make_async_copy(out_ref.at[rows], out_hbm.at[rows], out_sem.at[k])
        c.start()
        return c

    wqg_t[0:W] = turned(wq_ref[...])
    wqg_t[W:] = turned(wg_ref[...])
    cross(0)
    cross(1)
    send_rows(0)
    send_rows(1)
    spread(0)
    spread(1)
    send_rows(2)
    send_rows(3)
    wv_t[...] = turned(wv_ref[...])
    gb_t[...] = jnp.broadcast_to(gb_ref[...], (W, W)).T
    lax.fori_loop(0, ROWS // 4, own_step, 0)
    for k in range(4, CHUNKS):
        send_rows(k)
    pick(0)
    pick(1)
    rows_ready(0)
    rows_ready(1)
    rows_used(0)
    lay_out(0)
    lay_out(1)
    writes = []
    for k in range(CHUNKS):
        if k:
            rows_used(k)
        if k and k + 1 < CHUNKS:
            rows_ready(k + 1)
        attend(k * RC // 2, (k + 1) * RC // 2)
        if k:
            writes.append(write(k - 1))
    writes.append(write(CHUNKS - 1))

    for c in writes:
        c.wait()
    for c in sent:
        c.wait_send()


def per_device(
    pair_blocks, kept_pairs, owner, norm_gain, norm_offset, w_query, w_key, w_value, w_gate, gate_bias, w_bias, w_out
):
    hbm = pl.BlockSpec(memory_space=pltpu.HBM)
    dma = pltpu.SemaphoreType.DMA
    operands = (
        pair_blocks[0], kept_pairs.T, owner, norm_gain[None], norm_offset[None],
        w_query, w_key, w_value, w_gate, gate_bias[None], w_bias.T, w_out,
    )
    out = pl.pallas_call(
        kernel,
        out_shape=jax.ShapeDtypeStruct((ROWS, W, W), BF),
        in_specs=[hbm] * len(operands),
        out_specs=hbm,
        scratch_shapes=[
            (pltpu.SMEM if o.dtype == I32 else pltpu.VMEM)(o.shape, o.dtype) for o in operands
        ]
        + [pltpu.VMEM((ROWS, W, W), BF)]
        + [pltpu.VMEM((2, NY, KL, W), BF)] * PARTS
        + [pltpu.VMEM((7, 2, KL, W), BF)] * PARTS
        + [pltpu.VMEM((NZ, 2, KL, W), BF)] * PARTS
        + [pltpu.VMEM((2, KL, W), BF)] * PARTS
        + [pltpu.VMEM((NX, 2, KL, W), BF)] * PARTS
        + [
            pltpu.VMEM((PARTS, KL, W), BF),
            pltpu.VMEM((NX, PARTS, KL, W), BF),
            pltpu.VMEM((ROWS, W, W), BF),
            pltpu.VMEM((ROWS, W, W), F32),
            pltpu.VMEM((ROWS, 3 * W, W), BF),
            pltpu.VMEM((ROWS, W, 3 * W), BF),
            pltpu.VMEM((ROWS, W, W), BF),
            pltpu.VMEM((ROWS, W, W), BF),
        ]
        + [pltpu.VMEM((3 * W, PH * W), F32)] * PARTS
        + [
            pltpu.VMEM((2 * W, W), BF),
            pltpu.VMEM((W, W), BF),
            pltpu.VMEM((W, W), F32),
            pltpu.VMEM((W, W), F32),
        ]
        + [pltpu.VMEM((2, 3 * W, PH * W), F32)] * 2
        + [pltpu.VMEM((2, 3 * W, PH * W), BF)] * 2
        + [pltpu.VMEM((2, 8, PH * W), F32)] * 2
        + [
            dma((len(operands),)), dma((CHUNKS,)),
            dma((PARTS, 7)), dma((PARTS, 7)), dma((PARTS,)), dma((PARTS,)), dma((PARTS, 7)), dma((PARTS, 7)),
            dma((3,)), dma((3,)), dma((PARTS, 3)), dma((PARTS, 3)), dma((CHUNKS, 4)), dma((CHUNKS, 4)),
        ]
        + [pltpu.VMEM((4, RC, W, W), BF)] * CHUNKS,
        compiler_params=pltpu.CompilerParams(
            collective_id=0, has_side_effects=True, vmem_limit_bytes=60 * 2**20
        ),
        name="row_attention",
    )(*operands)
    return out[None]


def solution(mesh):
    return jax.shard_map(
        per_device,
        mesh=mesh,
        in_specs=(P("blk", "rep", None, None),) + (P(),) * 11,
        out_specs=P("blk", "rep", None, None),
        check_vma=False,
    )
```

```python
import functools

import jax
import jax.numpy as jnp
from jax import lax
from jax.experimental import pallas as pl
from jax.experimental.pallas import tpu as pltpu
from jax.sharding import PartitionSpec as P

F32 = jnp.float32
BF = jnp.bfloat16
I32 = jnp.int32
MESH = pl.DeviceIdType.MESH
LOG2E = 1.4426950408889634
MASKED = -1e30

NZ, NY, NX = 8, 8, 4
PLANE = 2 * NY
KEPT = NZ * PLANE
ROWS = 32
W = 128
HEADS, HD = 4, 32
CHUNKS = 8
PARTS = 2
PH = HEADS // PARTS
KL = W // PARTS
RC = ROWS // CHUNKS
STEPS = (4, 3, -3, 2, -2, 1, -1)
X_STEPS = (2, 1, -1)


def dot(a, b):
    return jnp.dot(a, b, preferred_element_type=F32)


def dot_nt(a, b):
    return lax.dot_general(a, b, (((1,), (1,)), ((), ())), preferred_element_type=F32)


def dot_tn(a, b):
    return lax.dot_general(a, b, (((0,), (0,)), ((), ())), preferred_element_type=F32)


def norm_rows(x, gain, offset):
    v = x.astype(F32)
    d = v - jnp.mean(v, axis=-1, keepdims=True)
    s = jnp.mean(d * d, axis=-1, keepdims=True)
    return (d * lax.rsqrt(s + 1e-05) * gain + offset).astype(BF)


def row_members(kept, slot):
    row = kept[0, slot]

    def same(step):
        other = slot + step
        inside = (other >= 0) & (other < KEPT)
        return inside & (kept[0, jnp.clip(other, 0, KEPT - 1)] == row)

    m1, m2, p1, p2 = same(-1), same(-2), same(1), same(2)
    first = jnp.where(m1, -1, 1)
    second = jnp.where(m1 & p1, 1, jnp.where(m2, -2, 2))
    return first, m1 | p1, second, (m1 & p1) | m2 | p2


def bias_wants(kept, owner, slot):
    first, has_first, second, has_second = row_members(kept, slot)
    col = kept[1, slot]
    k1 = kept[1, jnp.clip(slot + first, 0, KEPT - 1)]
    k2 = kept[1, jnp.clip(slot + second, 0, KEPT - 1)]
    g0 = owner[col, col]
    g1 = jnp.where(has_first, owner[col, k1], -1)
    g2 = jnp.where(has_second, owner[col, k2], -1)
    diag = kept[0, slot] == col
    one = jnp.where(diag, g1, g0)
    two = jnp.where(diag, g2, jnp.maximum(g1, g2))
    return diag, g0, g1, g2, one, two


def kernel(
    x_hbm, kept_hbm, owner_hbm, gain_hbm, offset_hbm, wq_hbm, wk_hbm, wv_hbm, wg_hbm, gb_hbm, wb_hbm, wo_hbm,
    out_hbm,
    x_ref, kept, owner, gain_ref, offset_ref, wq_ref, wk_ref, wv_ref, wg_ref, gb_ref, wb_ref, wo_ref,
    normed, plane0, plane1, z_send0, z_send1, z_recv0, z_recv1, picked0, picked1, whole0, whole1,
    own_piece, whole_own, q_t, gate_t, k_all, v_t, gated, out_ref, bias0, bias1, wqg_t, wv_t, gb_t, wb_rep,
    s0, s1, p0, p1, m0, m1,
    in_sem, out_sem, y_ss, y_rs, c_ss, c_rs, z_ss, z_rs, o_ss, o_rs, x_ss, x_rs, n_ss, n_rs, *nbs
):
    blk = lax.axis_index("blk")
    rep = lax.axis_index("rep")
    z = blk // PLANE
    y = (blk // 2) % NY
    core = blk % 2
    planes, z_sends, z_recvs = (plane0, plane1), (z_send0, z_send1), (z_recv0, z_recv1)
    pickeds, wholes, biases = (picked0, picked1), (whole0, whole1), (bias0, bias1)

    def at_blk(b):
        return {"blk": (b + KEPT) % KEPT}

    def at_y(step):
        return {"blk": z * PLANE + ((y + step + NY) % NY) * 2 + core}

    def at_z(step):
        return {"blk": ((z + step + NZ) % NZ) * PLANE + y * 2 + core}

    def at_x(step):
        return {"rep": (rep + step + NX) % NX}

    mate = {"blk": blk + 1 - 2 * core}

    barrier = pltpu.get_barrier_semaphore()
    greeted = [at_y(s) for s in STEPS] + [at_z(s) for s in STEPS] + [at_x(s) for s in X_STEPS] + [mate]
    greeted += [at_blk(blk - 2), at_blk(blk + 2)]
    for device in greeted:
        pl.semaphore_signal(barrier, inc=1, device_id=device, device_id_type=MESH)

    operands = (x_hbm, kept_hbm, owner_hbm, gain_hbm, offset_hbm, wq_hbm, wk_hbm, wv_hbm, wg_hbm, gb_hbm, wb_hbm, wo_hbm)
    places = (x_ref, kept, owner, gain_ref, offset_ref, wq_ref, wk_ref, wv_ref, wg_ref, gb_ref, wb_ref, wo_ref)
    fetches = [pltpu.make_async_copy(o, p, in_sem.at[n]) for n, (o, p) in enumerate(zip(operands, places))]
    for c in fetches:
        c.start()
    for n in (0, 3, 4, 10):
        fetches[n].wait()

    def remote(src, dst, ss, rs, device):
        return pltpu.make_async_remote_copy(
            src_ref=src, dst_ref=dst, send_sem=ss, recv_sem=rs, device_id=device, device_id_type=MESH
        )

    def turned(w):
        return w.astype(F32).T.astype(BF)

    wb = jnp.broadcast_to(wb_ref[...].astype(F32)[:, None], (HEADS, ROWS, W)).reshape(W, W)
    wb_rep[...] = wb.T

    lane = lax.broadcasted_iota(I32, (W, W), 1)

    def norm_step(t, piece):
        rows, cols = [], []
        for u in range(8):
            i = t * 8 + u
            n = norm_rows(x_ref[i], gain_ref[...], offset_ref[...])
            normed[i] = n
            rows.append(n)
            cols.append(jnp.where(lane % ROWS == i, wb_rep[...], 0.0).astype(BF))
        return piece + dot(jnp.concatenate(rows, axis=1), jnp.concatenate(cols, axis=0))

    sent = []

    def send_rows(k):
        src = normed.at[pl.ds(k * RC, RC)]
        for c in (
            remote(src, nbs[k].at[0], n_ss.at[k, 1], n_rs.at[k, 0], at_blk(blk + 2)),
            remote(src, nbs[k].at[3], n_ss.at[k, 2], n_rs.at[k, 3], at_blk(blk - 2)),
            remote(src, nbs[k].at[1 + core], n_ss.at[k, 0], n_rs.at[k, 1 + core], mate),
        ):
            c.start()
            sent.append(c)

    piece = lax.fori_loop(0, ROWS // 8, norm_step, jnp.zeros((W, W), F32))
    span = PH * ROWS
    place = lax.broadcasted_iota(I32, (KL, W), 1) // span
    for p in range(PARTS):
        packed = None
        for hi in range(PARTS):
            v = piece[hi * KL : (hi + 1) * KL]
            shift = ((hi - p) * span) % W
            v = pltpu.roll(v, shift, 1) if shift else v
            packed = v if packed is None else jnp.where(place == hi, v, packed)
        own_piece[p] = packed.astype(BF)
        planes[p][core, (y, z)[p]] = packed.astype(BF)

    gather_at, hand_at = (at_y, at_z), (at_z, at_y)
    gather_pos, hand_pos = (y, z), (z, y)

    def gather_index(p, slot):
        slot = lax.rem(slot + KEPT, KEPT)
        return lax.rem(slot // 2, NY) if p == 0 else slot // PLANE

    def hand_index(p, slot):
        return gather_index(1 - p, slot)

    pl.semaphore_wait(barrier, len(greeted))

    y_copies = [
        [
            remote(
                planes[p].at[core, gather_pos[p]], planes[p].at[core, gather_pos[p]],
                y_ss.at[p, n], y_rs.at[p, n], gather_at[p](s),
            )
            for n, s in enumerate(STEPS)
        ]
        for p in range(PARTS)
    ]
    for p in range(PARTS):
        for c in y_copies[p]:
            c.start()
            sent.append(c)
    for n, s in enumerate(X_STEPS):
        c = remote(own_piece, whole_own.at[rep], o_ss.at[n], o_rs.at[n], at_x(s))
        c.start()
        sent.append(c)
    whole_own[rep] = own_piece[...]

    for n in (1, 2, 5, 6, 7, 8, 9, 11):
        fetches[n].wait()
    wants = [
        [bias_wants(kept, owner, ((z + s + NZ) % NZ) * PLANE + y * 2 + core)[4:] for s in STEPS],
        [bias_wants(kept, owner, z * PLANE + ((y + s + NY) % NY) * 2 + core)[4:] for s in STEPS],
    ]
    diag, g0, g1, g2, one, two = bias_wants(kept, owner, blk)
    first, has_first, second, has_second = row_members(kept, blk)
    sel1 = jnp.where(first < 0, 1, 2)
    sel2 = jnp.where(second == -2, 0, jnp.where(second == 1, 2, 3))

    def cross(p):
        for c in y_copies[p]:
            c.wait_recv()
        c = remote(planes[p].at[core], planes[p].at[core], c_ss.at[p], c_rs.at[p], mate)
        c.start()
        sent.append(c)

    def spread(p):
        remote(planes[p].at[1 - core], planes[p].at[1 - core], c_ss.at[p], c_rs.at[p], mate).wait_recv()
        for n, s in enumerate(STEPS):
            for item, want in enumerate(wants[p][n]):
                z_sends[p][n, item] = planes[p][lax.rem(want + KEPT, 2), gather_index(p, want)]
            c = remote(z_sends[p].at[n], z_recvs[p].at[hand_pos[p]], z_ss.at[p, n], z_rs.at[p, n], hand_at[p](s))
            c.start()
            sent.append(c)
        for item, want in enumerate((one, two)):
            z_recvs[p][hand_pos[p], item] = planes[p][lax.rem(want + KEPT, 2), gather_index(p, want)]

    def pick(p):
        for n, s in enumerate(STEPS):
            there = (hand_pos[p] - s + NZ) % NZ
            remote(z_sends[p].at[n], z_recvs[p].at[there], z_ss.at[p, n], z_rs.at[p, n], hand_at[p](s)).wait_recv()
        pickeds[p][0] = z_recvs[p][hand_index(p, one), 0]
        pickeds[p][1] = z_recvs[p][hand_index(p, two), 1]
        for n, s in enumerate(X_STEPS):
            c = remote(pickeds[p], wholes[p].at[rep], x_ss.at[p, n], x_rs.at[p, n], at_x(s))
            c.start()
            sent.append(c)
        wholes[p][rep] = pickeds[p][...]

    group = lax.broadcasted_iota(I32, (KL, W), 1) // ROWS

    def lay_out(p):
        if p == 0:
            for n, s in enumerate(X_STEPS):
                remote(own_piece, whole_own.at[(rep - s + NX) % NX], o_ss.at[n], o_rs.at[n], at_x(s)).wait_recv()
        for n, s in enumerate(X_STEPS):
            remote(
                pickeds[p], wholes[p].at[(rep - s + NX) % NX], x_ss.at[p, n], x_rs.at[p, n], at_x(s)
            ).wait_recv()
        owns = [whole_own[r, p].astype(F32) * LOG2E for r in range(NX)]
        ones = [wholes[p][r, 0].astype(F32) * LOG2E for r in range(NX)]
        twos = [wholes[p][r, 1].astype(F32) * LOG2E for r in range(NX)]
        for t in range(3):
            if t == 0:
                parts = [jnp.where(diag, a, b) for a, b in zip(owns, ones)]
            if t == 1:
                blank = jnp.where(has_first, 0.0, MASKED)
                parts = [jnp.where(g1 >= 0, jnp.where(diag, a, b), blank) for a, b in zip(ones, twos)]
            if t == 2:
                blank = jnp.where(has_second, 0.0, MASKED)
                parts = [jnp.where(g2 >= 0, b, blank) for b in twos]
            for hi in range(PARTS):
                for h in range(PH):
                    acc = None
                    for r in range(NX):
                        shift = ((r - hi * PH - h) * ROWS) % W
                        v = pltpu.roll(parts[r], shift, 1) if shift else parts[r]
                        acc = v if acc is None else jnp.where(group == r, v, acc)
                    biases[p][t * W + hi * KL : t * W + (hi + 1) * KL, h * W : (h + 1) * W] = acc

    def own_step(t, _):
        for u in range(4):
            i = t * 4 + u
            n = normed[i]
            qg = dot_nt(wqg_t[...], n)
            q_t[i] = (qg[:W] * (HD**-0.5 * LOG2E)).astype(BF)
            gate_t[i] = jax.nn.sigmoid(qg[W:] + gb_t[...])
            k_all[i, 0:W] = dot(n, wk_ref[...]).astype(BF)
            v_t[i, :, 0:W] = dot_nt(wv_t[...], n).astype(BF)
        return 0

    def rows_ready(k):
        src = normed.at[pl.ds(k * RC, RC)]
        for slot in (0, 3):
            remote(src, nbs[k].at[slot], n_ss.at[k, 1], n_rs.at[k, slot], mate).wait_recv()
        c = remote(nbs[k].at[3 - 3 * core], nbs[k].at[2 - core], n_ss.at[k, 3], n_rs.at[k, 2 - core], mate)
        c.start()
        sent.append(c)

    def rows_used(k):
        src = normed.at[pl.ds(k * RC, RC)]
        for slot in (2 - core, 1 + core):
            remote(src, nbs[k].at[slot], n_ss.at[k, 0], n_rs.at[k, slot], mate).wait_recv()

        def key_step(t, _):
            for u in range(4):
                j = t * 4 + u
                i = k * RC + j
                both = jnp.concatenate([nbs[k][sel1, j], nbs[k][sel2, j]], axis=0)
                k_all[i, W:] = dot(both, wk_ref[...]).astype(BF)
                v_t[i, :, W:] = dot_nt(wv_t[...], both).astype(BF)
            return 0

        lax.fori_loop(0, RC // 4, key_step, 0)

    row_head = lax.broadcasted_iota(I32, (W, W), 0) // HD

    def score_stage(p, rr, s_ref, m_ref):
        for u in range(2):
            q = q_t[rr * 2 + u]
            q_diag = jnp.concatenate(
                [jnp.where(row_head == h, q, jnp.zeros_like(q)) for h in range(p * PH, (p + 1) * PH)], axis=1
            )
            s = dot(k_all[rr * 2 + u], q_diag) + biases[p][...]
            s_ref[u] = s
            m_ref[u] = jnp.max(s.reshape(48, 8, PH * W), axis=0)

    def weight_stage(s_ref, m_ref, p_ref):
        for u in range(2):
            for h in range(PH):
                cols = slice(h * W, (h + 1) * W)
                top = jnp.max(m_ref[u, :, cols], axis=0, keepdims=True)
                p_ref[u, :, cols] = jnp.exp2(s_ref[u, :, cols] - top).astype(BF)

    def value_stage(p, rr, p_ref):
        heads = slice(p * PH * HD, (p + 1) * PH * HD)
        ones = jnp.ones((16, 3 * W), BF)
        for u in range(2):
            i = rr * 2 + u
            r = dot(jnp.concatenate([v_t[i, heads], ones], axis=0), p_ref[u])
            outs = []
            for h in range(PH):
                cols = slice(h * W, (h + 1) * W)
                outs.append(r[h * HD : (h + 1) * HD, cols] * (1.0 / r[PH * HD : PH * HD + 1, cols]))
            gated[i, heads] = (jnp.concatenate(outs, axis=0) * gate_t[i, heads]).astype(BF)

    def step(rr, before=True, here=True):
        if before:
            value_stage(0, rr - 1, p0)
            weight_stage(s1, m1, p1)
        if here:
            score_stage(0, rr, s0, m0)
        if before:
            value_stage(1, rr - 1, p1)
        if here:
            weight_stage(s0, m0, p0)
            score_stage(1, rr, s1, m1)

    def attend(lo, hi):
        def row_step(rr, _):
            step(rr)
            return 0

        if lo == 0:
            step(0, before=False)
        lax.fori_loop(max(lo, 1), hi, row_step, 0)
        if hi == ROWS // 2:
            step(hi, here=False)

    def write(k):
        for i in range(k * RC, (k + 1) * RC):
            out_ref[i] = dot_tn(gated[i], wo_ref[...]).astype(BF)
        rows = pl.ds(k * RC, RC)
        c = pltpu.make_async_copy(out_ref.at[rows], out_hbm.at[rows], out_sem.at[k])
        c.start()
        return c

    wqg_t[0:W] = turned(wq_ref[...])
    wqg_t[W:] = turned(wg_ref[...])
    cross(0)
    cross(1)
    send_rows(0)
    send_rows(1)
    spread(0)
    spread(1)
    send_rows(2)
    send_rows(3)
    wv_t[...] = turned(wv_ref[...])
    gb_t[...] = jnp.broadcast_to(gb_ref[...], (W, W)).T
    lax.fori_loop(0, ROWS // 4, own_step, 0)
    for k in range(4, CHUNKS):
        send_rows(k)
    pick(0)
    pick(1)
    rows_ready(0)
    rows_ready(1)
    rows_used(0)
    lay_out(0)
    lay_out(1)
    writes = []
    for k in range(CHUNKS):
        if k:
            rows_used(k)
        if k and k + 1 < CHUNKS:
            rows_ready(k + 1)
        attend(k * RC // 2, (k + 1) * RC // 2)
        if k:
            writes.append(write(k - 1))
    writes.append(write(CHUNKS - 1))

    for c in writes:
        c.wait()
    for c in sent:
        c.wait_send()


def per_device(
    pair_blocks, kept_pairs, owner, norm_gain, norm_offset, w_query, w_key, w_value, w_gate, gate_bias, w_bias, w_out
):
    hbm = pl.BlockSpec(memory_space=pltpu.HBM)
    dma = pltpu.SemaphoreType.DMA
    operands = (
        pair_blocks[0], kept_pairs.T, owner, norm_gain[None], norm_offset[None],
        w_query, w_key, w_value, w_gate, gate_bias[None], w_bias.T, w_out,
    )
    out = pl.pallas_call(
        kernel,
        out_shape=jax.ShapeDtypeStruct((ROWS, W, W), BF),
        in_specs=[hbm] * len(operands),
        out_specs=hbm,
        scratch_shapes=[
            (pltpu.SMEM if o.dtype == I32 else pltpu.VMEM)(o.shape, o.dtype) for o in operands
        ]
        + [pltpu.VMEM((ROWS, W, W), BF)]
        + [pltpu.VMEM((2, NY, KL, W), BF)] * PARTS
        + [pltpu.VMEM((7, 2, KL, W), BF)] * PARTS
        + [pltpu.VMEM((NZ, 2, KL, W), BF)] * PARTS
        + [pltpu.VMEM((2, KL, W), BF)] * PARTS
        + [pltpu.VMEM((NX, 2, KL, W), BF)] * PARTS
        + [
            pltpu.VMEM((PARTS, KL, W), BF),
            pltpu.VMEM((NX, PARTS, KL, W), BF),
            pltpu.VMEM((ROWS, W, W), BF),
            pltpu.VMEM((ROWS, W, W), F32),
            pltpu.VMEM((ROWS, 3 * W, W), BF),
            pltpu.VMEM((ROWS, W, 3 * W), BF),
            pltpu.VMEM((ROWS, W, W), BF),
            pltpu.VMEM((ROWS, W, W), BF),
        ]
        + [pltpu.VMEM((3 * W, PH * W), F32)] * PARTS
        + [
            pltpu.VMEM((2 * W, W), BF),
            pltpu.VMEM((W, W), BF),
            pltpu.VMEM((W, W), F32),
            pltpu.VMEM((W, W), F32),
        ]
        + [pltpu.VMEM((2, 3 * W, PH * W), F32)] * 2
        + [pltpu.VMEM((2, 3 * W, PH * W), BF)] * 2
        + [pltpu.VMEM((2, 8, PH * W), F32)] * 2
        + [
            dma((len(operands),)), dma((CHUNKS,)),
            dma((PARTS, 7)), dma((PARTS, 7)), dma((PARTS,)), dma((PARTS,)), dma((PARTS, 7)), dma((PARTS, 7)),
            dma((3,)), dma((3,)), dma((PARTS, 3)), dma((PARTS, 3)), dma((CHUNKS, 4)), dma((CHUNKS, 4)),
        ]
        + [pltpu.VMEM((4, RC, W, W), BF)] * CHUNKS,
        compiler_params=pltpu.CompilerParams(
            collective_id=0, has_side_effects=True, vmem_limit_bytes=60 * 2**20
        ),
        name="row_attention",
    )(*operands)
    return out[None]


def solution(mesh):
    return jax.shard_map(
        per_device,
        mesh=mesh,
        in_specs=(P("blk", "rep", None, None),) + (P(),) * 11,
        out_specs=P("blk", "rep", None, None),
        check_vma=False,
    )
```
